256 devices in a mesh: pb: 32 (over z_lo, x, core), kv: 8 (over z_hi, y).
Axes of the slice: x: 4, y: 4, z: 8 (z_hi: 2, z_lo: 4; z = z_hi * 4 + z_lo), core: 2. Of those that a mesh axis runs over, the one named last changes fastest.
Arguments:
- queries: bfloat16 [32768, 2048], P(('pb', 'kv')), may hold values from -120.20815 to 120.20815
- key_vectors: bfloat16 [32768, 512], P(('pb', 'kv')), may hold values from -4 to 4
- value_vectors: bfloat16 [32768, 512], P(('pb', 'kv')), may hold values from -6 to 6
- output_gradient: bfloat16 [32768, 2048], P(('pb', 'kv')), may hold values from -6 to 6
- doc_lengths: int32 [48], replicated, may hold values from 1 to 1024, 32768 in all
Outputs:
- query_grad: bfloat16 [32768, 2048], P(('pb', 'kv'))
- key_gradient: bfloat16 [32768, 512], P(('pb', 'kv'))
- value_gradient: bfloat16 [32768, 512], P(('pb', 'kv'))
The draws below stay inside these ranges and needn't reach their ends.
Inputs may be any that keep to these rules, and one draw needn't show every extreme that they name: `doc_lengths`: the 48 lengths sum to 32768; the longest is exactly 1024.
All inputs are finite; a program needn't handle non-finite values.
Results may differ from the reference program's by a relative error of at most 0.033.
Values may be sent and summed in bfloat16 or wider, within the bound.
A program may use at most 128 MiB of HBM per device.

```python
import math
import jax
import jax.numpy as jnp
import numpy as np
from jax import lax

QUERY_HEAD_COUNT = 16
KEY_VALUE_HEADS = 4
HEAD_WIDTH = 128
QUERIES_PER_KEY = 4
LOOK = 1
NDOC = 48
GROUP = 1024
PACK_TOKENS = 32768
DOC_MOST = 1024


def base_keys(key):
    return jnp.clip(jax.random.normal(key, (PACK_TOKENS, KEY_VALUE_HEADS * HEAD_WIDTH), jnp.float32), -4.0, 4.0)


def draw_key_vectors(key, part):
    shared_heads = base_keys(key)
    return shared_heads.astype(jnp.bfloat16)


def draw_queries(key, part):
    key = jax.random.fold_in(key, 12)
    fresh = jnp.clip(jax.random.normal(key, (PACK_TOKENS, QUERY_HEAD_COUNT * HEAD_WIDTH), jnp.float32), -6.0, 6.0)
    return fresh.astype(jnp.bfloat16)


def block_scale(rng, dims, split, low, largest):
    gain, own = 1.0, jax.random.fold_in(rng, 6)
    for position, parts in split:
        draws = jnp.exp(jax.random.uniform(jax.random.fold_in(own, position), (parts,), jnp.float32, low / len(split), largest / len(split)))
        gain = gain * jnp.repeat(draws, dims[position] // parts).reshape([-1 if axis == position else 1 for axis in range(len(dims))])
    return gain


def profile(amount, total, most, skew):
    loads = [(1 << 20) // math.isqrt(standing ** skew) + 1 for standing in range(2, amount + 1)]
    surplus, holding = total - most - (amount - 1), [1] * (amount - 1)
    while surplus > 0:
        free = [i for i in range(amount - 1) if holding[i] < most]
        mass, remaining = sum([loads[i] for i in free]), surplus
        for i in free:
            addition = min(most - holding[i], max(1, remaining * loads[i] // mass), surplus)
            holding[i] = holding[i] + addition
            surplus = surplus - addition
    return np.array([most] + holding)


def uneven(key, number_of, total, reach, skew):
    if number_of == 2:
        one = jax.random.randint(key, (), max(1, total - reach), min(reach, total - 1) + 1)
        return jnp.stack([one, total - one])
    lengths = jnp.asarray(profile(number_of, total, reach, skew), jnp.int32)
    pairs = (number_of - 1) // 2
    source_of, receiver = lengths[1:1 + 2 * pairs:2], lengths[2:2 + 2 * pairs:2]
    margin = jnp.minimum(source_of - 1, reach - receiver)
    shifted = jax.random.randint(jax.random.fold_in(key, 1), (pairs,), 0, 1 << 20) % (margin + 1)
    lengths = lengths.at[1:1 + 2 * pairs:2].set(source_of - shifted).at[2:2 + 2 * pairs:2].set(receiver + shifted)
    return lengths[jax.random.permutation(jax.random.fold_in(key, 2), number_of)]


def normal_values(rng, dims, scale, reach, pieces=(), kind=jnp.bfloat16):
    values = jax.random.normal(rng, dims, jnp.float32) * scale
    if len(pieces) > 0:
        values = block_scale(rng, dims, pieces, -0.22, 0.18) * values
    return jnp.clip(values, min=-reach, max=reach).astype(kind)


def setup_inputs(seed: int = 0) -> dict:
    streams_of = jax.random.split(jax.random.key(seed), 6)
    queries = draw_queries(jax.random.fold_in(streams_of[5], 71), 0)
    key_vectors = draw_key_vectors(jax.random.fold_in(streams_of[5], 71), 0)
    value_vectors = normal_values(streams_of[2], (PACK_TOKENS, KEY_VALUE_HEADS * HEAD_WIDTH), 1.0, 6.0, ((0, 256),))
    output_gradient = normal_values(streams_of[3], (PACK_TOKENS, QUERY_HEAD_COUNT * HEAD_WIDTH), 1.0, 6.0, ((0, 256),))
    doc_lengths = uneven(streams_of[4], NDOC, PACK_TOKENS, DOC_MOST, 2).astype(jnp.int32)
    return dict(queries=queries, key_vectors=key_vectors, value_vectors=value_vectors, output_gradient=output_gradient, doc_lengths=doc_lengths)


NEG_FILL = -1.0e30


def doc_index(positions, doc_ends):
    return jnp.sum((positions[:, None] >= doc_ends[None, :]).astype(jnp.int32), axis=1)


def reference(queries, key_vectors, value_vectors, output_gradient, doc_lengths):
    token_span = LOOK * GROUP
    width = token_span + GROUP
    logit_scale = HEAD_WIDTH ** -0.5
    doc_ends = jnp.cumsum(doc_lengths).astype(jnp.int32)
    all_positions = jnp.arange(PACK_TOKENS + token_span, dtype=jnp.int32) - token_span
    all_docs = doc_index(all_positions, doc_ends)
    padding_rows = jnp.zeros((token_span, KEY_VALUE_HEADS, HEAD_WIDTH), jnp.float32)
    full_keys = jnp.concatenate([padding_rows, key_vectors.astype(jnp.float32).reshape(PACK_TOKENS, KEY_VALUE_HEADS, HEAD_WIDTH)], axis=0)
    full_values = jnp.concatenate([padding_rows, value_vectors.astype(jnp.float32).reshape(PACK_TOKENS, KEY_VALUE_HEADS, HEAD_WIDTH)], axis=0)
    full_queries = queries.astype(jnp.float32).reshape(PACK_TOKENS, KEY_VALUE_HEADS, QUERIES_PER_KEY, HEAD_WIDTH)
    full_gradient = output_gradient.astype(jnp.float32).reshape(PACK_TOKENS, KEY_VALUE_HEADS, QUERIES_PER_KEY, HEAD_WIDTH)

    def one_group(carry, index):
        summed_key_grad, summed_value_grad = carry
        start = (index * GROUP).astype(jnp.int32)
        query_block = lax.dynamic_slice_in_dim(full_queries, start, GROUP, 0)
        grad_block = lax.dynamic_slice_in_dim(full_gradient, start, GROUP, 0)
        key_block = lax.dynamic_slice_in_dim(full_keys, start, width, 0)
        value_block = lax.dynamic_slice_in_dim(full_values, start, width, 0)
        query_positions = start + jnp.arange(GROUP, dtype=jnp.int32)
        query_docs = lax.dynamic_slice_in_dim(all_docs, start + token_span, GROUP, 0)
        key_positions = lax.dynamic_slice_in_dim(all_positions, start, width, 0)
        key_docs = lax.dynamic_slice_in_dim(all_docs, start, width, 0)
        allowed = (key_positions[None, :] <= query_positions[:, None]) & (key_docs[None, :] == query_docs[:, None]) & (key_positions[None, :] >= 0)
        scores = jnp.einsum("qgcd,kgd->gcqk", query_block, key_block) * logit_scale
        logits = jnp.where(allowed, scores, NEG_FILL)
        row_max = jnp.max(logits, axis=-1, keepdims=True)
        row_sum = jnp.sum(jnp.where(allowed, jnp.exp(logits - row_max), 0.0), axis=-1, keepdims=True)
        log_total = row_max + jnp.log(row_sum)
        probs = jnp.exp(jnp.where(allowed, scores - log_total, NEG_FILL))
        probs_low = lax.optimization_barrier(probs.astype(jnp.bfloat16)).astype(jnp.float32)
        attended = jnp.einsum("gcqk,kgd->qgcd", probs_low, value_block)
        row_delta = jnp.einsum("qgcd,qgcd->gcq", grad_block, attended)
        prob_grad = jnp.einsum("qgcd,kgd->gcqk", grad_block, value_block)
        score_grad = lax.optimization_barrier((probs * (prob_grad - row_delta[..., None])).astype(jnp.bfloat16)).astype(jnp.float32)
        query_part = jnp.einsum("gcqk,kgd->qgcd", score_grad, key_block) * logit_scale
        key_part = jnp.einsum("gcqk,qgcd->kgd", score_grad, query_block)
        value_part = jnp.einsum("gcqk,qgcd->kgd", probs_low, grad_block)
        summed_key_grad = lax.dynamic_update_slice_in_dim(summed_key_grad, lax.dynamic_slice_in_dim(summed_key_grad, start, width, 0) + key_part, start, 0)
        summed_value_grad = lax.dynamic_update_slice_in_dim(summed_value_grad, lax.dynamic_slice_in_dim(summed_value_grad, start, width, 0) + value_part, start, 0)
        return (summed_key_grad, summed_value_grad), query_part.reshape(GROUP, QUERY_HEAD_COUNT * HEAD_WIDTH).astype(jnp.bfloat16)

    zeroed_sum = jnp.zeros((PACK_TOKENS + token_span, KEY_VALUE_HEADS, HEAD_WIDTH), jnp.float32)
    (summed_key_grad, summed_value_grad), query_blocks = lax.scan(one_group, (zeroed_sum, zeroed_sum), jnp.arange(PACK_TOKENS // GROUP, dtype=jnp.int32))
    query_grad = query_blocks.reshape(PACK_TOKENS, QUERY_HEAD_COUNT * HEAD_WIDTH)
    key_gradient = (summed_key_grad[token_span:] * logit_scale).reshape(PACK_TOKENS, KEY_VALUE_HEADS * HEAD_WIDTH).astype(jnp.bfloat16)
    value_gradient = summed_value_grad[token_span:].reshape(PACK_TOKENS, KEY_VALUE_HEADS * HEAD_WIDTH).astype(jnp.bfloat16)
    return (query_grad, key_gradient, value_gradient)
```

```python
import functools

import jax
import jax.numpy as jnp
from jax import lax
from jax.experimental import pallas as pl
from jax.experimental.pallas import tpu as pltpu
from jax.sharding import PartitionSpec as P

MESH = pl.DeviceIdType.MESH
HEADS = 4
SHARE = 4
WIDTH = 128
BLOCK = 128
HALF = HEADS * BLOCK
NEAR = 5 * BLOCK
PAIR = 2 * WIDTH
HALVES = 64
UNITS = 8
SCALE = WIDTH**-0.5
RATE = SCALE * 1.4426950408889634
FILL = -1e30


def contract_last(left, right):
    return lax.dot_general(left, right, (((1,), (1,)), ((), ())), preferred_element_type=jnp.float32)


def matmul(left, right):
    return jnp.dot(left, right, preferred_element_type=jnp.float32)


def heads_to_rows(x):
    return jnp.concatenate([x[:, :WIDTH], x[:, WIDTH:]], axis=0)


def fold(x, op):
    return op(x.reshape(x.shape[0] // 8, 8, x.shape[1]), axis=0)


def wait(ref, sem):
    pltpu.make_async_copy(ref, ref, sem).wait()


def kernel(
    q_ref, k_ref, v_ref, g_ref, len_ref,
    dq_ref, dk_ref, dv_ref,
    kv, own_in, far_in, old_in, kt, qg0, qg1, starts, e1, p1, e2, p2, ds2, ds1, stat, dqt, acc1, acc2, dqs0, dqs1, far_out, relay_out, relay_in, own_out, back,
    send, own_sem, far_sem, old_sem, q_sem, relay_sem, back_sem, dq_sem,
):
    pb, column = lax.axis_index("pb"), lax.axis_index("kv")
    half = 2 * pb + column // HEADS
    y = lax.rem(column, HEADS)

    def place(shift, row):
        there = lax.rem(half + shift + HALVES, HALVES)
        return (there // 2, lax.rem(there, 2) * HEADS + row)

    def row_at(step):
        return lax.rem(y + step, HEADS)

    partners = [place(0, row_at(d)) for d in (1, 2, 3)]
    partners += [place(s, row_at(d)) for s in (1, -1) for d in range(HEADS)]
    partners += [place(2, y), place(-2, y)]
    barrier = pltpu.get_barrier_semaphore()
    for device in partners:
        pl.semaphore_signal(barrier, inc=1, device_id=device, device_id_type=MESH)

    positions = (
        lax.broadcasted_iota(jnp.int32, (8, WIDTH), 0) * BLOCK
        + lax.broadcasted_iota(jnp.int32, (8, WIDTH), 1)
        + half * HALF
    )

    def count(i, carry):
        end, start = carry
        end = end + len_ref[i]
        return end, jnp.where(positions >= end, end, start)

    _, doc_start = lax.fori_loop(
        0, len_ref.shape[0], count, (jnp.int32(0), jnp.zeros((8, WIDTH), jnp.int32))
    )
    starts[...] = doc_start - half * HALF
    acc1[...] = jnp.zeros_like(acc1)
    acc2[...] = jnp.zeros_like(acc2)
    pl.semaphore_wait(barrier, len(partners))

    started = []
    qg, dqs = (qg0, qg1), (dqs0, dqs1)

    def push(src, dst, send_sem, recv_sem, device):
        copy = pltpu.make_async_remote_copy(
            src_ref=src, dst_ref=dst, send_sem=send_sem, recv_sem=recv_sem, device_id=device, device_id_type=MESH
        )
        copy.start()
        return copy

    def push_one(src, dst, recv_sem, device):
        started.append(push(src, dst, send.at[len(started)], recv_sem, device))

    for d in range(HEADS):
        h = row_at(d)
        cols = pl.ds(pl.multiple_of(h * WIDTH, WIDTH), WIDTH)
        for part, ref in enumerate((k_ref, v_ref)):
            src = ref.at[:, cols]
            slot = pl.ds(pl.multiple_of(y * BLOCK, BLOCK), BLOCK)
            far, own = far_in.at[part, slot], own_in.at[part, slot]
            push_one(src, far, far_sem, place(1, h))
            if d == 0:
                pltpu.make_async_copy(src, own, own_sem).start()
            else:
                push_one(src, own, own_sem, place(0, h))
    for pair in range(2):
        for d in range(HEADS):
            h = row_at(d)
            cols = pl.ds(pl.multiple_of(h * SHARE * WIDTH + pair * PAIR, PAIR), PAIR)
            for part, ref in enumerate((q_ref, g_ref)):
                dst = qg[pair].at[y, part]
                sem = q_sem.at[pair]
                if d == 0:
                    pltpu.make_async_copy(ref.at[:, cols], dst, sem).start()
                else:
                    push_one(ref.at[:, cols], dst, sem, place(0, h))

    wait(own_in, own_sem)
    push_one(own_in, old_in, old_sem, place(2, y))
    kv[:, HALF : 2 * HALF] = own_in[...]
    kt[:, HALF : 2 * HALF] = own_in[0].T
    wait(old_in, old_sem)
    kv[:, 0:HALF] = old_in[...]
    kt[:, 0:HALF] = old_in[0].T

    row = lax.broadcasted_iota(jnp.int32, (BLOCK, PAIR), 0)
    token = lax.rem(lax.broadcasted_iota(jnp.int32, (BLOCK, PAIR), 1), WIDTH)

    def first_of(j):
        line = starts[pl.ds(j, 1)]
        return jnp.concatenate([line, line], axis=1)

    def scores(k_of, q, j, blocks, key_base, out, causal_last):
        first = first_of(j)
        top = jnp.full((8, PAIR), FILL, jnp.float32)
        for b in range(blocks):
            s = contract_last(k_of(b), q)
            keep = row >= first - key_base(b)
            if causal_last and b == blocks - 1:
                keep = keep & (row <= token)
            s = jnp.where(keep, s, FILL)
            out[b * BLOCK : (b + 1) * BLOCK] = s
            top = jnp.maximum(top, fold(s, jnp.max))
        return jnp.max(top, axis=0, keepdims=True)

    def weights(v_of, g, blocks, top, e_out, p_out):
        shift = top * RATE
        total = jnp.zeros((8, PAIR), jnp.float32)
        delta = jnp.zeros((8, PAIR), jnp.float32)
        for b in range(blocks):
            rows = slice(b * BLOCK, (b + 1) * BLOCK)
            e = jnp.exp2(e_out[rows] * RATE - shift)
            e_out[rows] = e
            p = contract_last(v_of(b), g)
            p_out[rows] = p
            total = total + fold(e, jnp.sum)
            delta = delta + fold(e * p, jnp.sum)
        return jnp.sum(total, axis=0, keepdims=True), jnp.sum(delta, axis=0, keepdims=True)

    def near_scores(pair, j, _):
        u = pair * HEADS + j
        q = heads_to_rows(qg[pair][j, 0])
        g = heads_to_rows(qg[pair][j, 1])

        def near_rows(part):
            return lambda b: kv[part, pl.ds(pl.multiple_of((j + b) * BLOCK, BLOCK), BLOCK)]

        def key_base(b):
            block = j + b
            return jnp.where(block < HEADS, block * BLOCK - 2 * HALF, (block - HEADS) * BLOCK)

        top = scores(near_rows(0), q, j, 5, key_base, e1.at[u], True)
        total, delta = weights(near_rows(1), g, 5, top, e1.at[u], p1.at[u])
        stat[u, 0:1] = top
        stat[u, 1:2] = total
        stat[u, 2:3] = delta
        return 0

    for pair in range(2):
        wait(qg[pair], q_sem.at[pair])
        lax.fori_loop(0, HEADS, functools.partial(near_scores, pair), 0)

    wait(far_in, far_sem)
    kt[:, 2 * HALF : 3 * HALF] = far_in[0].T

    def far_work(pair, j, _):
        u = pair * HEADS + j
        q = heads_to_rows(qg[pair][j, 0])
        g = heads_to_rows(qg[pair][j, 1])

        def far_rows(part):
            return lambda b: far_in[part, b * BLOCK : (b + 1) * BLOCK]

        top2 = scores(far_rows(0), q, j, 4, lambda b: b * BLOCK - HALF, e2, False)
        total2, delta2 = weights(far_rows(1), g, 4, top2, e2, p2)
        top1, total1, delta1 = stat[u, 0:1], stat[u, 1:2], stat[u, 2:3]
        top = jnp.maximum(top1, top2)
        a1 = jnp.exp2((top1 - top) * RATE)
        a2 = jnp.exp2((top2 - top) * RATE)
        inverse = 1.0 / (a1 * total1 + a2 * total2)
        delta = (a1 * delta1 + a2 * delta2) * inverse
        a2 = a2 * inverse
        stat[u, 0:1] = a1 * inverse
        stat[u, 1:2] = delta
        for b in range(4):
            rows = slice(b * BLOCK, (b + 1) * BLOCK)
            p = e2[rows] * a2
            ds = (p * (p2[rows] - delta)).astype(jnp.bfloat16)
            ds2[rows] = ds
            acc2[0, rows] += matmul(ds, q)
            acc2[1, rows] += matmul(p.astype(jnp.bfloat16), g)
        dqt[u] = matmul(kt[:, 2 * HALF : 3 * HALF], ds2[...])
        return 0

    for pair in range(2):
        lax.fori_loop(0, HEADS, functools.partial(far_work, pair), 0)

    far_out[...] = acc2[...].astype(jnp.bfloat16)
    mine = pl.ds(pl.multiple_of(y * WIDTH, WIDTH), WIDTH)
    for d in range(HEADS):
        j = row_at(d)
        rows = pl.ds(pl.multiple_of(j * BLOCK, BLOCK), BLOCK)
        push_one(far_out.at[:, rows], back.at[1, :, :, mine], back_sem.at[1], place(-1, j))

    def near_work(pair, j, _):
        u = pair * HEADS + j
        q = heads_to_rows(qg[pair][j, 0])
        g = heads_to_rows(qg[pair][j, 1])
        a1, delta = stat[u, 0:1], stat[u, 1:2]
        for b in range(5):
            rows = slice(b * BLOCK, (b + 1) * BLOCK)
            p = e1[u, rows] * a1
            ds = (p * (p1[u, rows] - delta)).astype(jnp.bfloat16)
            ds1[rows] = ds
            where = pl.ds(pl.multiple_of((j + b) * BLOCK, BLOCK), BLOCK)
            acc1[0, where] += matmul(ds, q)
            acc1[1, where] += matmul(p.astype(jnp.bfloat16), g)
        total = dqt[u] + matmul(kt[:, pl.ds(pl.multiple_of(j * BLOCK, BLOCK), NEAR)], ds1[...])
        total = (total * SCALE).T.astype(jnp.bfloat16)
        dqs[pair][j] = jnp.concatenate([total[:BLOCK], total[BLOCK:]], axis=1)
        return 0

    for pair in range(2):
        lax.fori_loop(0, HEADS, functools.partial(near_work, pair), 0)
        dst = dq_ref.at[:, pl.ds(pl.multiple_of(y * SHARE * WIDTH + pair * PAIR, PAIR), PAIR)]
        for d in range(HEADS):
            j = row_at(d)
            if d == 0:
                pltpu.make_async_copy(dqs[pair].at[j], dst, dq_sem).start()
            else:
                push_one(dqs[pair].at[j], dst, dq_sem, place(0, j))

    relay_out[...] = acc1[:, 0:HALF].astype(jnp.bfloat16)
    push_one(relay_out, relay_in, relay_sem, place(-2, y))
    wait(relay_in, relay_sem)
    own_out[...] = (acc1[:, HALF : 2 * HALF] + relay_in[...].astype(jnp.float32)).astype(jnp.bfloat16)
    for d in range(HEADS):
        j = row_at(d)
        rows = pl.ds(pl.multiple_of(j * BLOCK, BLOCK), BLOCK)
        if d == 0:
            pltpu.make_async_copy(own_out.at[:, rows], back.at[0, :, :, mine], back_sem.at[0]).start()
        else:
            push_one(own_out.at[:, rows], back.at[0, :, :, mine], back_sem.at[0], place(0, j))
    wait(back.at[0], back_sem.at[0])
    wait(back.at[1], back_sem.at[1])
    dk_ref[...] = ((back[0, 0].astype(jnp.float32) + back[1, 0].astype(jnp.float32)) * SCALE).astype(jnp.bfloat16)
    dv_ref[...] = (back[0, 1].astype(jnp.float32) + back[1, 1].astype(jnp.float32)).astype(jnp.bfloat16)
    wait(dq_ref, dq_sem)
    for copy in started:
        copy.wait_send()


def local(queries, key_vectors, value_vectors, output_gradient, doc_lengths):
    low, full = jnp.bfloat16, jnp.float32
    wide = jax.ShapeDtypeStruct((BLOCK, HEADS * SHARE * WIDTH), low)
    narrow = jax.ShapeDtypeStruct((BLOCK, HEADS * WIDTH), low)
    anywhere = pl.BlockSpec(memory_space=pl.ANY)
    near = pl.BlockSpec(memory_space=pltpu.VMEM)
    return pl.pallas_call(
        kernel,
        out_shape=(wide, narrow, narrow),
        in_specs=[anywhere] * 4 + [pl.BlockSpec(memory_space=pltpu.SMEM)],
        out_specs=(anywhere, near, near),
        scratch_shapes=[
            pltpu.VMEM((2, 2 * HALF, WIDTH), low),
            pltpu.VMEM((2, HALF, WIDTH), low),
            pltpu.VMEM((2, HALF, WIDTH), low),
            pltpu.VMEM((2, HALF, WIDTH), low),
            pltpu.VMEM((WIDTH, 3 * HALF), low),
            pltpu.VMEM((HEADS, 2, BLOCK, PAIR), low),
            pltpu.VMEM((HEADS, 2, BLOCK, PAIR), low),
            pltpu.VMEM((8, WIDTH), jnp.int32),
            pltpu.VMEM((UNITS, NEAR, PAIR), full),
            pltpu.VMEM((UNITS, NEAR, PAIR), full),
            pltpu.VMEM((HALF, PAIR), full),
            pltpu.VMEM((HALF, PAIR), full),
            pltpu.VMEM((HALF, PAIR), low),
            pltpu.VMEM((NEAR, PAIR), low),
            pltpu.VMEM((UNITS, 8, PAIR), full),
            pltpu.VMEM((UNITS, WIDTH, PAIR), full),
            pltpu.VMEM((2, 2 * HALF, WIDTH), full),
            pltpu.VMEM((2, HALF, WIDTH), full),
            pltpu.VMEM((HEADS, BLOCK, PAIR), low),
            pltpu.VMEM((HEADS, BLOCK, PAIR), low),
            pltpu.VMEM((2, HALF, WIDTH), low),
            pltpu.VMEM((2, HALF, WIDTH), low),
            pltpu.VMEM((2, HALF, WIDTH), low),
            pltpu.VMEM((2, HALF, WIDTH), low),
            pltpu.VMEM((2, 2, BLOCK, HEADS * WIDTH), low),
            pltpu.SemaphoreType.DMA((48,)),
            pltpu.SemaphoreType.DMA,
            pltpu.SemaphoreType.DMA,
            pltpu.SemaphoreType.DMA,
            pltpu.SemaphoreType.DMA((2,)),
            pltpu.SemaphoreType.DMA,
            pltpu.SemaphoreType.DMA((2,)),
            pltpu.SemaphoreType.DMA,
        ],
        compiler_params=pltpu.CompilerParams(
            collective_id=0, has_side_effects=True, vmem_limit_bytes=40 << 20
        ),
        cost_estimate=pl.CostEstimate(flops=3 << 30, bytes_accessed=3 << 20, transcendentals=3 << 20),
    )(queries, key_vectors, value_vectors, output_gradient, doc_lengths)


def solution(mesh):
    rows = P(("pb", "kv"), None)
    return jax.shard_map(
        local, mesh=mesh, in_specs=(rows, rows, rows, rows, P()), out_specs=(rows, rows, rows), check_vma=False
    )
```

```python
import functools

import jax
import jax.numpy as jnp
from jax import lax
from jax.experimental import pallas as pl
from jax.experimental.pallas import tpu as pltpu
from jax.sharding import PartitionSpec as P

MESH = pl.DeviceIdType.MESH
HEADS = 4
SHARE = 4
WIDTH = 128
BLOCK = 128
HALF = HEADS * BLOCK
NEAR = 5 * BLOCK
PAIR = 2 * WIDTH
HALVES = 64
CHUNK = 64
SCALE = WIDTH**-0.5
FILL = -1e30


def contract_last(left, right):
    return lax.dot_general(left, right, (((1,), (1,)), ((), ())), preferred_element_type=jnp.float32)


def matmul(left, right):
    return jnp.dot(left, right, preferred_element_type=jnp.float32)


def fold(x, op):
    return op(x.reshape(x.shape[0] // 8, 8, x.shape[1]), axis=0)


def wait(ref, sem):
    pltpu.make_async_copy(ref, ref, sem).wait()


def kernel(
    q_ref, k_ref, v_ref, g_ref, len_ref,
    dq_ref, dk_ref, dv_ref,
    kv, own_in, far_in, old_in, kt, kt_far, qg0, qg1, rows_of, starts,
    e1a, e1b, p1a, p1b, e2a, e2b, p2a, p2b, ds_far, pr_far, ds1a, ds1b, pr1a, pr1b,
    stat_a, stat_b, dqt_a, dqt_b, acc1, acc2, dqs0, dqs1, far_out, relay_out, relay_in, own_out, back,
    send, own_sem, far_sem, old_sem, q_sem, relay_sem, back_sem, dq_sem,
):
    qg, dqs, e1, p1, e2, p2 = (qg0, qg1), (dqs0, dqs1), (e1a, e1b), (p1a, p1b), (e2a, e2b), (p2a, p2b)
    ds1, pr1, stat, dqt = (ds1a, ds1b), (pr1a, pr1b), (stat_a, stat_b), (dqt_a, dqt_b)
    pb, column = lax.axis_index("pb"), lax.axis_index("kv")
    half = 2 * pb + column // HEADS
    y = lax.rem(column, HEADS)
    has_old = half >= 2
    has_later = half < HALVES - 2

    def place(shift, row):
        there = lax.rem(half + shift + HALVES, HALVES)
        return (there // 2, lax.rem(there, 2) * HEADS + row)

    def row_at(step):
        return lax.rem(y + step, HEADS)

    partners = [place(0, row_at(d)) for d in (1, 2, 3)]
    partners += [place(s, row_at(d)) for s in (1, -1) for d in range(HEADS)]
    barrier = pltpu.get_barrier_semaphore()
    for device in partners:
        pl.semaphore_signal(barrier, inc=1, device_id=device, device_id_type=MESH)

    @pl.when(has_later)
    def _():
        pl.semaphore_signal(barrier, inc=1, device_id=place(2, y), device_id_type=MESH)

    @pl.when(has_old)
    def _():
        pl.semaphore_signal(barrier, inc=1, device_id=place(-2, y), device_id_type=MESH)

    positions = (
        lax.broadcasted_iota(jnp.int32, (8, WIDTH), 0) * BLOCK
        + lax.broadcasted_iota(jnp.int32, (8, WIDTH), 1)
        + half * HALF
    )

    def count(i, carry):
        end, start = carry
        end = end + len_ref[i]
        return end, jnp.where(positions >= end, end, start)

    _, doc_start = lax.fori_loop(
        0, len_ref.shape[0], count, (jnp.int32(0), jnp.zeros((8, WIDTH), jnp.int32))
    )
    starts[...] = doc_start - half * HALF
    acc1[...] = jnp.zeros_like(acc1)

    @pl.when(jnp.logical_not(has_old))
    def _():
        old_in[...] = jnp.zeros_like(old_in)

    @pl.when(jnp.logical_not(has_later))
    def _():
        relay_in[...] = jnp.zeros_like(relay_in)

    pl.semaphore_wait(barrier, len(partners) + has_old.astype(jnp.int32) + has_later.astype(jnp.int32))

    started = []

    def remote(src, dst, send_sem, recv_sem, device):
        return pltpu.make_async_remote_copy(
            src_ref=src, dst_ref=dst, send_sem=send_sem, recv_sem=recv_sem, device_id=device, device_id_type=MESH
        )

    def push(src, dst, recv_sem, device):
        copy = remote(src, dst, send.at[len(started)], recv_sem, device)
        copy.start()
        started.append(copy)

    for part, ref in enumerate((k_ref, v_ref)):
        for d in range(HEADS):
            h = row_at(d)
            src = ref.at[:, pl.ds(pl.multiple_of(h * WIDTH, WIDTH), WIDTH)]
            slot = pl.ds(pl.multiple_of(y * BLOCK, BLOCK), BLOCK)
            push(src, far_in.at[part, slot], far_sem, place(1, h))
            if d == 0:
                pltpu.make_async_copy(src, own_in.at[part, slot], own_sem).start()
            else:
                push(src, own_in.at[part, slot], own_sem, place(0, h))
    for pair in range(2):
        for part, ref in enumerate((q_ref, g_ref)):
            for d in range(HEADS):
                h = row_at(d)
                cols = pl.ds(pl.multiple_of(h * SHARE * WIDTH + pair * PAIR, PAIR), PAIR)
                dst = qg[pair].at[y, part]
                if d == 0:
                    pltpu.make_async_copy(ref.at[:, cols], dst, q_sem.at[pair]).start()
                else:
                    push(ref.at[:, cols], dst, q_sem.at[pair], place(0, h))

    wait(own_in, own_sem)
    forward = remote(own_in, old_in, send.at[46], old_sem, place(2, y))

    @pl.when(has_later)
    def _():
        forward.start()

    kv[:, HALF : 2 * HALF] = own_in[...]
    kt[:, HALF : 2 * HALF] = own_in[0].T

    @pl.when(has_old)
    def _():
        wait(old_in, old_sem)

    kv[:, 0:HALF] = old_in[...]
    kt[:, 0:HALF] = old_in[0].T

    row = lax.broadcasted_iota(jnp.int32, (CHUNK, PAIR), 0)
    token = lax.rem(lax.broadcasted_iota(jnp.int32, (CHUNK, PAIR), 1), WIDTH)

    def unpack(pair):
        for j in range(HEADS):
            for part in range(2):
                x = qg[pair][j, part]
                rows_of[pair, part, j * PAIR : (j + 1) * PAIR] = jnp.concatenate([x[:, :WIDTH], x[:, WIDTH:]], axis=0)

    def unit(pair, i, k):
        j = 2 * i + k
        rows = pl.ds(pl.multiple_of(j * PAIR, PAIR), PAIR)
        return j, 2 * pair + i, rows_of[pair, 0, rows], rows_of[pair, 1, rows]

    def first_of(j):
        line = starts[pl.ds(j, 1)]
        return jnp.concatenate([line, line], axis=1)

    def softmax(first, chunks, base, e, p, diagonal):
        top = jnp.full((8, PAIR), FILL, jnp.float32)
        for c in range(chunks):
            rows = slice(c * CHUNK, (c + 1) * CHUNK)
            keep = row >= first - base(c)
            if diagonal and c >= chunks - BLOCK // CHUNK:
                keep = keep & (row + (c * CHUNK) % BLOCK <= token)
            s = jnp.where(keep, e[rows], FILL)
            e[rows] = s
            top = jnp.maximum(top, fold(s, jnp.max))
        top = jnp.max(top, axis=0, keepdims=True)
        total = jnp.zeros((8, PAIR), jnp.float32)
        delta = jnp.zeros((8, PAIR), jnp.float32)
        for c in range(chunks):
            rows = slice(c * CHUNK, (c + 1) * CHUNK)
            x = jnp.exp((e[rows] - top) * SCALE)
            e[rows] = x
            total = total + fold(x, jnp.sum)
            delta = delta + fold(x * p[rows], jnp.sum)
        return top, jnp.sum(total, axis=0, keepdims=True), jnp.sum(delta, axis=0, keepdims=True)

    def near_scores(pair, i, _):
        units = [unit(pair, i, k) for k in range(2)]
        for k, (j, u, q, g) in enumerate(units):
            keys = pl.ds(pl.multiple_of(j * BLOCK, BLOCK), NEAR)
            e1[k][u] = contract_last(kv[0, keys], q)
            p1[k][u] = contract_last(kv[1, keys], g)
        for k, (j, u, q, g) in enumerate(units):

            def base(c):
                block = j + c * CHUNK // BLOCK
                start = jnp.where(block < HEADS, block * BLOCK - 2 * HALF, (block - HEADS) * BLOCK)
                return start + (c * CHUNK) % BLOCK

            top, total, delta = softmax(first_of(j), NEAR // CHUNK, base, e1[k].at[u], p1[k].at[u], True)
            stat[k][u, 0:1] = top
            stat[k][u, 1:2] = total
            stat[k][u, 2:3] = delta
        return 0

    def far_work(pair, i, _):
        units = [unit(pair, i, k) for k in range(2)]
        for k, (j, u, q, g) in enumerate(units):
            e2[k][...] = contract_last(far_in[0], q)
            p2[k][...] = contract_last(far_in[1], g)
        for k, (j, u, q, g) in enumerate(units):
            top2, total2, delta2 = softmax(first_of(j), HALF // CHUNK, lambda c: c * CHUNK - HALF, e2[k], p2[k], False)
            top1, total1, delta1 = stat[k][u, 0:1], stat[k][u, 1:2], stat[k][u, 2:3]
            top = jnp.maximum(top1, top2)
            a1 = jnp.exp((top1 - top) * SCALE)
            a2 = jnp.exp((top2 - top) * SCALE)
            inverse = 1.0 / (a1 * total1 + a2 * total2)
            delta = (a1 * delta1 + a2 * delta2) * inverse
            a2 = a2 * inverse
            stat[k][u, 0:1] = a1 * inverse
            stat[k][u, 1:2] = delta
            cols = pl.ds(pl.multiple_of(j * PAIR, PAIR), PAIR)
            for c in range(HALF // CHUNK):
                rows = slice(c * CHUNK, (c + 1) * CHUNK)
                p = e2[k][rows] * a2
                ds_far[rows, cols] = (p * (p2[k][rows] - delta)).astype(jnp.bfloat16)
                pr_far[rows, cols] = p.astype(jnp.bfloat16)
        for k, (j, u, q, g) in enumerate(units):
            cols = pl.ds(pl.multiple_of(j * PAIR, PAIR), PAIR)
            dqt[k][u] = matmul(kt_far[...], ds_far[:, cols])
        return 0

    def near_work(pair, i, _):
        units = [unit(pair, i, k) for k in range(2)]
        for k, (j, u, q, g) in enumerate(units):
            a1, delta = stat[k][u, 0:1], stat[k][u, 1:2]
            for c in range(NEAR // CHUNK):
                rows = slice(c * CHUNK, (c + 1) * CHUNK)
                p = e1[k][u, rows] * a1
                ds1[k][rows] = (p * (p1[k][u, rows] - delta)).astype(jnp.bfloat16)
                pr1[k][rows] = p.astype(jnp.bfloat16)
        for k, (j, u, q, g) in enumerate(units):
            keys = pl.ds(pl.multiple_of(j * BLOCK, BLOCK), NEAR)
            acc1[0, keys] += matmul(ds1[k][...], q)
            acc1[1, keys] += matmul(pr1[k][...], g)
            total = dqt[k][u] + matmul(kt[:, keys], ds1[k][...])
            total = (total * SCALE).T.astype(jnp.bfloat16)
            dqs[pair][j] = jnp.concatenate([total[:BLOCK], total[BLOCK:]], axis=1)
        return 0

    def loop(body, pair):
        lax.fori_loop(0, 2, functools.partial(body, pair), 0)

    for pair in range(2):
        wait(qg[pair], q_sem.at[pair])
        unpack(pair)
        loop(near_scores, pair)
        if pair == 0:
            wait(far_in, far_sem)
            kt_far[...] = far_in[0].T
        loop(far_work, pair)
        dk_far = matmul(ds_far[...], rows_of[pair, 0])
        dv_far = matmul(pr_far[...], rows_of[pair, 1])
        if pair == 0:
            acc2[0] = dk_far
            acc2[1] = dv_far
        else:
            far_out[0] = (acc2[0] + dk_far).astype(jnp.bfloat16)
            far_out[1] = (acc2[1] + dv_far).astype(jnp.bfloat16)

    mine = pl.ds(pl.multiple_of(y * WIDTH, WIDTH), WIDTH)
    for d in range(HEADS):
        j = row_at(d)
        rows = pl.ds(pl.multiple_of(j * BLOCK, BLOCK), BLOCK)
        push(far_out.at[:, rows], back.at[1, :, :, mine], back_sem.at[1], place(-1, j))

    for pair in range(2):
        loop(near_work, pair)
        dst = dq_ref.at[:, pl.ds(pl.multiple_of(y * SHARE * WIDTH + pair * PAIR, PAIR), PAIR)]
        for d in range(HEADS):
            j = row_at(d)
            if d == 0:
                pltpu.make_async_copy(dqs[pair].at[j], dst, dq_sem).start()
            else:
                push(dqs[pair].at[j], dst, dq_sem, place(0, j))

    relay_out[...] = acc1[:, 0:HALF].astype(jnp.bfloat16)
    backward = remote(relay_out, relay_in, send.at[47], relay_sem, place(-2, y))

    @pl.when(has_old)
    def _():
        backward.start()

    @pl.when(has_later)
    def _():
        wait(relay_in, relay_sem)

    own_out[...] = (acc1[:, HALF : 2 * HALF] + relay_in[...].astype(jnp.float32)).astype(jnp.bfloat16)
    for d in range(HEADS):
        j = row_at(d)
        rows = pl.ds(pl.multiple_of(j * BLOCK, BLOCK), BLOCK)
        if d == 0:
            pltpu.make_async_copy(own_out.at[:, rows], back.at[0, :, :, mine], back_sem.at[0]).start()
        else:
            push(own_out.at[:, rows], back.at[0, :, :, mine], back_sem.at[0], place(0, j))
    wait(back.at[0], back_sem.at[0])
    wait(back.at[1], back_sem.at[1])
    dk_ref[...] = ((back[0, 0].astype(jnp.float32) + back[1, 0].astype(jnp.float32)) * SCALE).astype(jnp.bfloat16)
    dv_ref[...] = (back[0, 1].astype(jnp.float32) + back[1, 1].astype(jnp.float32)).astype(jnp.bfloat16)
    wait(dq_ref, dq_sem)
    for copy in started:
        copy.wait_send()

    @pl.when(has_later)
    def _():
        forward.wait_send()

    @pl.when(has_old)
    def _():
        backward.wait_send()


def local(queries, key_vectors, value_vectors, output_gradient, doc_lengths):
    low, full = jnp.bfloat16, jnp.float32
    wide = jax.ShapeDtypeStruct((BLOCK, HEADS * SHARE * WIDTH), low)
    narrow = jax.ShapeDtypeStruct((BLOCK, HEADS * WIDTH), low)
    anywhere = pl.BlockSpec(memory_space=pl.ANY)
    near = pl.BlockSpec(memory_space=pltpu.VMEM)
    return pl.pallas_call(
        kernel,
        out_shape=(wide, narrow, narrow),
        in_specs=[anywhere] * 4 + [pl.BlockSpec(memory_space=pltpu.SMEM)],
        out_specs=(anywhere, near, near),
        scratch_shapes=[
            pltpu.VMEM((2, 2 * HALF, WIDTH), low),
            pltpu.VMEM((2, HALF, WIDTH), low),
            pltpu.VMEM((2, HALF, WIDTH), low),
            pltpu.VMEM((2, HALF, WIDTH), low),
            pltpu.VMEM((WIDTH, 2 * HALF), low),
            pltpu.VMEM((WIDTH, HALF), low),
            pltpu.VMEM((HEADS, 2, BLOCK, PAIR), low),
            pltpu.VMEM((HEADS, 2, BLOCK, PAIR), low),
            pltpu.VMEM((2, 2, HEADS * PAIR, WIDTH), low),
            pltpu.VMEM((8, WIDTH), jnp.int32),
            pltpu.VMEM((4, NEAR, PAIR), full),
            pltpu.VMEM((4, NEAR, PAIR), full),
            pltpu.VMEM((4, NEAR, PAIR), full),
            pltpu.VMEM((4, NEAR, PAIR), full),
            pltpu.VMEM((HALF, PAIR), full),
            pltpu.VMEM((HALF, PAIR), full),
            pltpu.VMEM((HALF, PAIR), full),
            pltpu.VMEM((HALF, PAIR), full),
            pltpu.VMEM((HALF, HEADS * PAIR), low),
            pltpu.VMEM((HALF, HEADS * PAIR), low),
            pltpu.VMEM((NEAR, PAIR), low),
            pltpu.VMEM((NEAR, PAIR), low),
            pltpu.VMEM((NEAR, PAIR), low),
            pltpu.VMEM((NEAR, PAIR), low),
            pltpu.VMEM((4, 8, PAIR), full),
            pltpu.VMEM((4, 8, PAIR), full),
            pltpu.VMEM((4, WIDTH, PAIR), full),
            pltpu.VMEM((4, WIDTH, PAIR), full),
            pltpu.VMEM((2, 2 * HALF, WIDTH), full),
            pltpu.VMEM((2, HALF, WIDTH), full),
            pltpu.VMEM((HEADS, BLOCK, PAIR), low),
            pltpu.VMEM((HEADS, BLOCK, PAIR), low),
            pltpu.VMEM((2, HALF, WIDTH), low),
            pltpu.VMEM((2, HALF, WIDTH), low),
            pltpu.VMEM((2, HALF, WIDTH), low),
            pltpu.VMEM((2, HALF, WIDTH), low),
            pltpu.VMEM((2, 2, BLOCK, HEADS * WIDTH), low),
            pltpu.SemaphoreType.DMA((48,)),
            pltpu.SemaphoreType.DMA,
            pltpu.SemaphoreType.DMA,
            pltpu.SemaphoreType.DMA,
            pltpu.SemaphoreType.DMA((2,)),
            pltpu.SemaphoreType.DMA,
            pltpu.SemaphoreType.DMA((2,)),
            pltpu.SemaphoreType.DMA,
        ],
        compiler_params=pltpu.CompilerParams(
            collective_id=0, has_side_effects=True, vmem_limit_bytes=60 << 20
        ),
        cost_estimate=pl.CostEstimate(flops=3 << 30, bytes_accessed=3 << 20, transcendentals=3 << 20),
    )(queries, key_vectors, value_vectors, output_gradient, doc_lengths)


def solution(mesh):
    rows = P(("pb", "kv"), None)
    return jax.shard_map(
        local, mesh=mesh, in_specs=(rows, rows, rows, rows, P()), out_specs=(rows, rows, rows), check_vma=False
    )
```

```python
import functools

import jax
import jax.numpy as jnp
from jax import lax
from jax.experimental import pallas as pl
from jax.experimental.pallas import tpu as pltpu
from jax.sharding import PartitionSpec as P

MESH = pl.DeviceIdType.MESH
HEADS = 4
SHARE = 4
WIDTH = 128
BLOCK = 128
HALF = HEADS * BLOCK
NEAR = 5 * BLOCK
PAIR = 2 * WIDTH
HALVES = 64
CHUNK = 64
SCALE = WIDTH**-0.5
FILL = -1e30


def contract_last(left, right):
    return lax.dot_general(left, right, (((1,), (1,)), ((), ())), preferred_element_type=jnp.float32)


def matmul(left, right):
    return jnp.dot(left, right, preferred_element_type=jnp.float32)


def fold(x, op):
    return op(x.reshape(x.shape[0] // 8, 8, x.shape[1]), axis=0)


def wait(ref, sem):
    pltpu.make_async_copy(ref, ref, sem).wait()


def kernel(
    q_ref, k_ref, v_ref, g_ref, len_ref,
    dq_ref, back,
    kv, own_in, far_k, far_v, old_in, kt, kt_far, q0, g0, q1, g1, rows_of, starts,
    e1a, e1b, p1a, p1b, e2a, e2b, p2a, p2b, ds_fa, ds_fb, pr_fa, pr_fb, ds1a, ds1b, pr1a, pr1b,
    stat_a, stat_b, dqt_a, dqt_b, acc1, acc2, dqs0, dqs1, far_out, relay_out, relay_in, own_out,
    send, own_sem, far_sem, old_sem, q_sem, relay_sem, back_sem, dq_sem,
):
    qg, dqs, e1, p1, e2, p2 = ((q0, g0), (q1, g1)), (dqs0, dqs1), (e1a, e1b), (p1a, p1b), (e2a, e2b), (p2a, p2b)
    ds1, pr1, stat, dqt = (ds1a, ds1b), (pr1a, pr1b), (stat_a, stat_b), (dqt_a, dqt_b)
    ds_far, pr_far = (ds_fa, ds_fb), (pr_fa, pr_fb)
    pb, column = lax.axis_index("pb"), lax.axis_index("kv")
    half = 2 * pb + column // HEADS
    y = lax.rem(column, HEADS)
    has_old = half >= 2
    has_later = half < HALVES - 2

    def place(shift, row):
        there = lax.rem(half + shift + HALVES, HALVES)
        return (there // 2, lax.rem(there, 2) * HEADS + row)

    def row_at(step):
        return lax.rem(y + step, HEADS)

    partners = [place(0, row_at(d)) for d in (1, 2, 3)]
    partners += [place(s, row_at(d)) for s in (1, -1) for d in range(HEADS)]
    barrier = pltpu.get_barrier_semaphore()
    for device in partners:
        pl.semaphore_signal(barrier, inc=1, device_id=device, device_id_type=MESH)

    @pl.when(has_later)
    def _():
        pl.semaphore_signal(barrier, inc=1, device_id=place(2, y), device_id_type=MESH)

    @pl.when(has_old)
    def _():
        pl.semaphore_signal(barrier, inc=1, device_id=place(-2, y), device_id_type=MESH)

    positions = (
        lax.broadcasted_iota(jnp.int32, (8, WIDTH), 0) * BLOCK
        + lax.broadcasted_iota(jnp.int32, (8, WIDTH), 1)
        + half * HALF
    )

    def count(i, carry):
        end, start = carry
        end = end + len_ref[i]
        return end, jnp.where(positions >= end, end, start)

    _, doc_start = lax.fori_loop(
        0, len_ref.shape[0], count, (jnp.int32(0), jnp.zeros((8, WIDTH), jnp.int32))
    )
    starts[...] = doc_start - half * HALF
    acc1[...] = jnp.zeros_like(acc1)

    @pl.when(jnp.logical_not(has_old))
    def _():
        old_in[...] = jnp.zeros_like(old_in)

    @pl.when(jnp.logical_not(has_later))
    def _():
        relay_in[...] = jnp.zeros_like(relay_in)

    pl.semaphore_wait(barrier, len(partners) + has_old.astype(jnp.int32) + has_later.astype(jnp.int32))

    started = []

    def remote(src, dst, send_sem, recv_sem, device):
        return pltpu.make_async_remote_copy(
            src_ref=src, dst_ref=dst, send_sem=send_sem, recv_sem=recv_sem, device_id=device, device_id_type=MESH
        )

    def push(src, dst, recv_sem, device):
        copy = remote(src, dst, send.at[len(started)], recv_sem, device)
        copy.start()
        started.append(copy)

    for part, ref in enumerate((k_ref, v_ref)):
        for d in range(HEADS):
            h = row_at(d)
            src = ref.at[:, pl.ds(pl.multiple_of(h * WIDTH, WIDTH), WIDTH)]
            slot = pl.ds(pl.multiple_of(y * BLOCK, BLOCK), BLOCK)
            if part == 0:
                push(src, far_k.at[slot], far_sem.at[0], place(1, h))
            if d == 0:
                pltpu.make_async_copy(src, own_in.at[part, slot], own_sem).start()
            else:
                push(src, own_in.at[part, slot], own_sem, place(0, h))
    for pair in range(2):
        for part, ref in enumerate((q_ref, g_ref)):
            for d in range(HEADS):
                h = row_at(d)
                cols = pl.ds(pl.multiple_of(h * SHARE * WIDTH + pair * PAIR, PAIR), PAIR)
                dst, sem = qg[pair][part].at[y], q_sem.at[2 * pair + part]
                if d == 0:
                    pltpu.make_async_copy(ref.at[:, cols], dst, sem).start()
                else:
                    push(ref.at[:, cols], dst, sem, place(0, h))

    wait(own_in, own_sem)
    forward = remote(own_in, old_in, send.at[46], old_sem, place(2, y))

    @pl.when(has_later)
    def _():
        forward.start()

    push(own_in.at[1], far_v, far_sem.at[1], place(1, y))
    kv[:, HALF : 2 * HALF] = own_in[...]
    kt[:, HALF : 2 * HALF] = own_in[0].T

    @pl.when(has_old)
    def _():
        wait(old_in, old_sem)

    kv[:, 0:HALF] = old_in[...]
    kt[:, 0:HALF] = old_in[0].T

    row = lax.broadcasted_iota(jnp.int32, (CHUNK, PAIR), 0)
    token = lax.rem(lax.broadcasted_iota(jnp.int32, (CHUNK, PAIR), 1), WIDTH)

    def unpack(pair, part):
        wait(qg[pair][part], q_sem.at[2 * pair + part])
        for j in range(HEADS):
            x = qg[pair][part][j]
            rows = slice(j // 2 * PAIR, (j // 2 + 1) * PAIR)
            rows_of[pair, part, j % 2, rows] = jnp.concatenate([x[:, :WIDTH], x[:, WIDTH:]], axis=0)

    def units(pair, i):
        rows = pl.ds(pl.multiple_of(i * PAIR, PAIR), PAIR)
        return [(k, 2 * i + k, 2 * pair + i, rows_of.at[pair, 0, k, rows], rows_of.at[pair, 1, k, rows]) for k in range(2)]

    def first_of(j):
        line = starts[pl.ds(j, 1)]
        return jnp.concatenate([line, line], axis=1)

    def softmax(first, chunks, base, e, diagonal):
        top = jnp.full((8, PAIR), FILL, jnp.float32)
        for c in range(chunks):
            rows = slice(c * CHUNK, (c + 1) * CHUNK)
            keep = row >= first - base(c)
            if diagonal and c >= chunks - BLOCK // CHUNK:
                keep = keep & (row + (c * CHUNK) % BLOCK <= token)
            s = jnp.where(keep, e[rows], FILL)
            e[rows] = s
            top = jnp.maximum(top, fold(s, jnp.max))
        top = jnp.max(top, axis=0, keepdims=True)
        total = jnp.zeros((8, PAIR), jnp.float32)
        for c in range(chunks):
            rows = slice(c * CHUNK, (c + 1) * CHUNK)
            x = jnp.exp((e[rows] - top) * SCALE)
            e[rows] = x
            total = total + fold(x, jnp.sum)
        return top, jnp.sum(total, axis=0, keepdims=True)

    def weighted(chunks, e, p):
        delta = jnp.zeros((8, PAIR), jnp.float32)
        for c in range(chunks):
            rows = slice(c * CHUNK, (c + 1) * CHUNK)
            delta = delta + fold(e[rows] * p[rows], jnp.sum)
        return jnp.sum(delta, axis=0, keepdims=True)

    def near_scores(pair, i, _):
        for k, j, u, q, g in units(pair, i):
            keys = pl.ds(pl.multiple_of(j * BLOCK, BLOCK), NEAR)
            e1[k][u] = contract_last(kv[0, keys], q[...])
        for k, j, u, q, g in units(pair, i):

            def base(c):
                block = j + c * CHUNK // BLOCK
                start = jnp.where(block < HEADS, block * BLOCK - 2 * HALF, (block - HEADS) * BLOCK)
                return start + (c * CHUNK) % BLOCK

            top, total = softmax(first_of(j), NEAR // CHUNK, base, e1[k].at[u], True)
            stat[k][u, 0:1] = top
            stat[k][u, 1:2] = total
        return 0

    def far_scores(pair, i, _):
        for k, j, u, q, g in units(pair, i):
            e2[k][i] = contract_last(far_k[...], q[...])
        for k, j, u, q, g in units(pair, i):
            top, total = softmax(first_of(j), HALF // CHUNK, lambda c: c * CHUNK - HALF, e2[k].at[i], False)
            stat[k][u, 2:3] = top
            stat[k][u, 3:4] = total
        return 0

    def near_values(pair, i, _):
        for k, j, u, q, g in units(pair, i):
            keys = pl.ds(pl.multiple_of(j * BLOCK, BLOCK), NEAR)
            p1[k][u] = contract_last(kv[1, keys], g[...])
        for k, j, u, q, g in units(pair, i):
            stat[k][u, 4:5] = weighted(NEAR // CHUNK, e1[k].at[u], p1[k].at[u])
        return 0

    def far_values(pair, i, _):
        cols = pl.ds(pl.multiple_of(i * PAIR, PAIR), PAIR)
        for k, j, u, q, g in units(pair, i):
            p2[k][...] = contract_last(far_v[...], g[...])
        for k, j, u, q, g in units(pair, i):
            delta2 = weighted(HALF // CHUNK, e2[k].at[i], p2[k])
            top1, total1, top2, total2, delta1 = [stat[k][u, n : n + 1] for n in range(5)]
            top = jnp.maximum(top1, top2)
            a1 = jnp.exp((top1 - top) * SCALE)
            a2 = jnp.exp((top2 - top) * SCALE)
            inverse = 1.0 / (a1 * total1 + a2 * total2)
            delta = (a1 * delta1 + a2 * delta2) * inverse
            a2 = a2 * inverse
            stat[k][u, 5:6] = a1 * inverse
            stat[k][u, 6:7] = delta
            for c in range(HALF // CHUNK):
                rows = slice(c * CHUNK, (c + 1) * CHUNK)
                p = e2[k][i, rows] * a2
                ds_far[k][rows, cols] = (p * (p2[k][rows] - delta)).astype(jnp.bfloat16)
                pr_far[k][rows, cols] = p.astype(jnp.bfloat16)
        return 0

    def far_queries(pair, i, _):
        cols = pl.ds(pl.multiple_of(i * PAIR, PAIR), PAIR)
        for k, j, u, q, g in units(pair, i):
            dqt[k][u] = matmul(kt_far[...], ds_far[k][:, cols])
        return 0

    def near_work(pair, i, _):
        for k, j, u, q, g in units(pair, i):
            a1, delta = stat[k][u, 5:6], stat[k][u, 6:7]
            for c in range(NEAR // CHUNK):
                rows = slice(c * CHUNK, (c + 1) * CHUNK)
                p = e1[k][u, rows] * a1
                ds1[k][rows] = (p * (p1[k][u, rows] - delta)).astype(jnp.bfloat16)
                pr1[k][rows] = p.astype(jnp.bfloat16)
        for k, j, u, q, g in units(pair, i):
            keys = pl.ds(pl.multiple_of(j * BLOCK, BLOCK), NEAR)
            acc1[0, keys] += matmul(ds1[k][...], q[...])
            acc1[1, keys] += matmul(pr1[k][...], g[...])
            total = dqt[k][u] + matmul(kt[:, keys], ds1[k][...])
            total = (total * SCALE).T.astype(jnp.bfloat16)
            dqs[pair][j] = jnp.concatenate([total[:BLOCK], total[BLOCK:]], axis=1)
        return 0

    def loop(body, pair):
        lax.fori_loop(0, 2, functools.partial(body, pair), 0)

    for pair in range(2):
        unpack(pair, 0)
        loop(near_scores, pair)
        if pair == 0:
            unpack(pair, 1)
            loop(near_values, pair)
            wait(far_k, far_sem.at[0])
            kt_far[...] = far_k[...].T
            loop(far_scores, pair)
            wait(far_v, far_sem.at[1])
        else:
            loop(far_scores, pair)
            unpack(pair, 1)
            loop(near_values, pair)
        loop(far_values, pair)
        if pair == 0:
            loop(far_queries, pair)
        dk_far = matmul(ds_fa[...], rows_of[pair, 0, 0]) + matmul(ds_fb[...], rows_of[pair, 0, 1])
        dv_far = matmul(pr_fa[...], rows_of[pair, 1, 0]) + matmul(pr_fb[...], rows_of[pair, 1, 1])
        if pair == 0:
            acc2[0] = dk_far
            acc2[1] = dv_far
        else:
            far_out[0] = (acc2[0] + dk_far).astype(jnp.bfloat16)
            far_out[1] = (acc2[1] + dv_far).astype(jnp.bfloat16)

    mine = pl.ds(pl.multiple_of(y * WIDTH, WIDTH), WIDTH)
    for d in range(HEADS):
        j = row_at(d)
        rows = pl.ds(pl.multiple_of(j * BLOCK, BLOCK), BLOCK)
        push(far_out.at[:, rows], back.at[1, :, :, mine], back_sem.at[1], place(-1, j))

    loop(far_queries, 1)
    for pair in range(2):
        loop(near_work, pair)
        dst = dq_ref.at[:, pl.ds(pl.multiple_of(y * SHARE * WIDTH + pair * PAIR, PAIR), PAIR)]
        for d in range(HEADS):
            j = row_at(d)
            if d == 0:
                pltpu.make_async_copy(dqs[pair].at[j], dst, dq_sem).start()
            else:
                push(dqs[pair].at[j], dst, dq_sem, place(0, j))

    relay_out[...] = acc1[:, 0:HALF].astype(jnp.bfloat16)
    backward = remote(relay_out, relay_in, send.at[47], relay_sem, place(-2, y))

    @pl.when(has_old)
    def _():
        backward.start()

    @pl.when(has_later)
    def _():
        wait(relay_in, relay_sem)

    own_out[...] = (acc1[:, HALF : 2 * HALF] + relay_in[...].astype(jnp.float32)).astype(jnp.bfloat16)
    for d in range(HEADS):
        j = row_at(d)
        rows = pl.ds(pl.multiple_of(j * BLOCK, BLOCK), BLOCK)
        if d == 0:
            pltpu.make_async_copy(own_out.at[:, rows], back.at[0, :, :, mine], back_sem.at[0]).start()
        else:
            push(own_out.at[:, rows], back.at[0, :, :, mine], back_sem.at[0], place(0, j))
    wait(back.at[0], back_sem.at[0])
    wait(back.at[1], back_sem.at[1])
    wait(dq_ref, dq_sem)
    for copy in started:
        copy.wait_send()

    @pl.when(has_later)
    def _():
        forward.wait_send()

    @pl.when(has_old)
    def _():
        backward.wait_send()


def finish(dq_in, back, dq_ref, dk_ref, dv_ref):
    dq_ref[...] = dq_in[...]
    total = back[0].astype(jnp.float32) + back[1].astype(jnp.float32)
    dk_ref[...] = (total[0] * SCALE).astype(jnp.bfloat16)
    dv_ref[...] = total[1].astype(jnp.bfloat16)


def local(queries, key_vectors, value_vectors, output_gradient, doc_lengths):
    low, full = jnp.bfloat16, jnp.float32
    wide = jax.ShapeDtypeStruct((BLOCK, HEADS * SHARE * WIDTH), low)
    narrow = jax.ShapeDtypeStruct((BLOCK, HEADS * WIDTH), low)
    shares = jax.ShapeDtypeStruct((2, 2, BLOCK, HEADS * WIDTH), low)
    anywhere = pl.BlockSpec(memory_space=pl.ANY)
    near = pl.BlockSpec(memory_space=pltpu.VMEM)
    query_grad, back = pl.pallas_call(
        kernel,
        out_shape=(wide, shares),
        in_specs=[anywhere] * 4 + [pl.BlockSpec(memory_space=pltpu.SMEM)],
        out_specs=(anywhere, anywhere),
        scratch_shapes=[
            pltpu.VMEM((2, 2 * HALF, WIDTH), low),
            pltpu.VMEM((2, HALF, WIDTH), low),
            pltpu.VMEM((HALF, WIDTH), low),
            pltpu.VMEM((HALF, WIDTH), low),
            pltpu.VMEM((2, HALF, WIDTH), low),
            pltpu.VMEM((WIDTH, 2 * HALF), low),
            pltpu.VMEM((WIDTH, HALF), low),
            pltpu.VMEM((HEADS, BLOCK, PAIR), low),
            pltpu.VMEM((HEADS, BLOCK, PAIR), low),
            pltpu.VMEM((HEADS, BLOCK, PAIR), low),
            pltpu.VMEM((HEADS, BLOCK, PAIR), low),
            pltpu.VMEM((2, 2, 2, 2 * PAIR, WIDTH), low),
            pltpu.VMEM((8, WIDTH), jnp.int32),
            pltpu.VMEM((4, NEAR, PAIR), full),
            pltpu.VMEM((4, NEAR, PAIR), full),
            pltpu.VMEM((4, NEAR, PAIR), full),
            pltpu.VMEM((4, NEAR, PAIR), full),
            pltpu.VMEM((2, HALF, PAIR), full),
            pltpu.VMEM((2, HALF, PAIR), full),
            pltpu.VMEM((HALF, PAIR), full),
            pltpu.VMEM((HALF, PAIR), full),
            pltpu.VMEM((HALF, 2 * PAIR), low),
            pltpu.VMEM((HALF, 2 * PAIR), low),
            pltpu.VMEM((HALF, 2 * PAIR), low),
            pltpu.VMEM((HALF, 2 * PAIR), low),
            pltpu.VMEM((NEAR, PAIR), low),
            pltpu.VMEM((NEAR, PAIR), low),
            pltpu.VMEM((NEAR, PAIR), low),
            pltpu.VMEM((NEAR, PAIR), low),
            pltpu.VMEM((4, 8, PAIR), full),
            pltpu.VMEM((4, 8, PAIR), full),
            pltpu.VMEM((4, WIDTH, PAIR), full),
            pltpu.VMEM((4, WIDTH, PAIR), full),
            pltpu.VMEM((2, 2 * HALF, WIDTH), full),
            pltpu.VMEM((2, HALF, WIDTH), full),
            pltpu.VMEM((HEADS, BLOCK, PAIR), low),
            pltpu.VMEM((HEADS, BLOCK, PAIR), low),
            pltpu.VMEM((2, HALF, WIDTH), low),
            pltpu.VMEM((2, HALF, WIDTH), low),
            pltpu.VMEM((2, HALF, WIDTH), low),
            pltpu.VMEM((2, HALF, WIDTH), low),
            pltpu.SemaphoreType.DMA((48,)),
            pltpu.SemaphoreType.DMA,
            pltpu.SemaphoreType.DMA((2,)),
            pltpu.SemaphoreType.DMA,
            pltpu.SemaphoreType.DMA((4,)),
            pltpu.SemaphoreType.DMA,
            pltpu.SemaphoreType.DMA((2,)),
            pltpu.SemaphoreType.DMA,
        ],
        compiler_params=pltpu.CompilerParams(
            collective_id=0, has_side_effects=True, vmem_limit_bytes=60 << 20
        ),
        cost_estimate=pl.CostEstimate(flops=3 << 30, bytes_accessed=3 << 20, transcendentals=3 << 20),
    )(queries, key_vectors, value_vectors, output_gradient, doc_lengths)
    return pl.pallas_call(
        finish,
        out_shape=(wide, narrow, narrow),
        in_specs=[near, near],
        out_specs=(near, near, near),
        compiler_params=pltpu.CompilerParams(vmem_limit_bytes=60 << 20),
    )(query_grad, back)


def solution(mesh):
    rows = P(("pb", "kv"), None)
    return jax.shard_map(
        local, mesh=mesh, in_specs=(rows, rows, rows, rows, P()), out_specs=(rows, rows, rows), check_vma=False
    )
```

```python
import jax
import jax.numpy as jnp
from jax import lax
from jax.experimental import pallas as pl
from jax.experimental.pallas import tpu as pltpu
from jax.sharding import PartitionSpec as P

MESH = pl.DeviceIdType.MESH
HEADS = 4
SHARE = 4
WIDTH = 128
BLOCK = 128
HALF = HEADS * BLOCK
NEAR = 5 * BLOCK
PAIR = 2 * WIDTH
HALVES = 64
CHUNK = 64
SCALE = WIDTH**-0.5
FILL = -1e30


def contract_last(left, right):
    return lax.dot_general(left, right, (((1,), (1,)), ((), ())), preferred_element_type=jnp.float32)


def matmul(left, right):
    return jnp.dot(left, right, preferred_element_type=jnp.float32)


def fold(x, op):
    return op(x.reshape(x.shape[0] // 8, 8, x.shape[1]), axis=0)


def wait(ref, sem):
    pltpu.make_async_copy(ref, ref, sem).wait()


def kernel(
    q_ref, k_ref, v_ref, g_ref, len_ref,
    dq_ref, back,
    kv, own_in, far_k, far_v, old_in, kt, kt_far, q0, g0, q1, g1, rows_of, starts,
    e1a, e1b, p1a, p1b, e2a, e2b, p2a, p2b, ds_fa, ds_fb, pr_fa, pr_fb, ds_0, ds_1, ds_2, ds_3, pr_0, pr_1, pr_2, pr_3,
    stat_a, stat_b, dqt_a, dqt_b, acc1, acc2, dqs0, dqs1, far_ok, far_ov, relay_out, relay_in, own_out,
    send, own_sem, far_sem, old_sem, q_sem, relay_sem, back_sem, dq_sem,
):
    dqs = (dqs0, dqs1)
    qg, e1, p1, e2, p2 = ((q0, g0), (q1, g1)), (e1a, e1b), (p1a, p1b), (e2a, e2b), (p2a, p2b)
    ds1, pr1 = (ds_0, ds_1, ds_2, ds_3), (pr_0, pr_1, pr_2, pr_3)
    stat, dqt = (stat_a, stat_b), (dqt_a, dqt_b)
    ds_far, pr_far, far_out = (ds_fa, ds_fb), (pr_fa, pr_fb), (far_ok, far_ov)
    pb, column = lax.axis_index("pb"), lax.axis_index("kv")
    half = 2 * pb + column // HEADS
    y = lax.rem(column, HEADS)
    has_old = half >= 2
    has_later = half < HALVES - 2

    def place(shift, row):
        there = lax.rem(half + shift + HALVES, HALVES)
        return (there // 2, lax.rem(there, 2) * HEADS + row)

    def row_at(step):
        return lax.rem(y + step, HEADS)

    partners = [place(0, row_at(d)) for d in (1, 2, 3)]
    partners += [place(s, row_at(d)) for s in (1, -1) for d in range(HEADS)]
    barrier = pltpu.get_barrier_semaphore()
    for device in partners:
        pl.semaphore_signal(barrier, inc=1, device_id=device, device_id_type=MESH)

    @pl.when(has_later)
    def _():
        pl.semaphore_signal(barrier, inc=1, device_id=place(2, y), device_id_type=MESH)

    @pl.when(has_old)
    def _():
        pl.semaphore_signal(barrier, inc=1, device_id=place(-2, y), device_id_type=MESH)

    pl.semaphore_wait(barrier, len(partners) + has_old.astype(jnp.int32) + has_later.astype(jnp.int32))

    started = []

    def remote(src, dst, send_sem, recv_sem, device):
        return pltpu.make_async_remote_copy(
            src_ref=src, dst_ref=dst, send_sem=send_sem, recv_sem=recv_sem, device_id=device, device_id_type=MESH
        )

    def push(src, dst, recv_sem, device):
        copy = remote(src, dst, send.at[len(started)], recv_sem, device)
        copy.start()
        started.append(copy)

    for part, ref in enumerate((k_ref, v_ref)):
        for d in range(HEADS):
            h = row_at(d)
            src = ref.at[:, pl.ds(pl.multiple_of(h * WIDTH, WIDTH), WIDTH)]
            slot = pl.ds(pl.multiple_of(y * BLOCK, BLOCK), BLOCK)
            if part == 0:
                push(src, far_k.at[slot], far_sem.at[0], place(1, h))
            if d == 0:
                pltpu.make_async_copy(src, own_in.at[part, slot], own_sem).start()
            else:
                push(src, own_in.at[part, slot], own_sem, place(0, h))
    for pair in range(2):
        for part, ref in enumerate((q_ref, g_ref)):
            for d in range(HEADS):
                h = row_at(d)
                cols = pl.ds(pl.multiple_of(h * SHARE * WIDTH + pair * PAIR, PAIR), PAIR)
                dst, sem = qg[pair][part].at[y], q_sem.at[2 * pair + part]
                if d == 0:
                    pltpu.make_async_copy(ref.at[:, cols], dst, sem).start()
                else:
                    push(ref.at[:, cols], dst, sem, place(0, h))

    positions = (
        lax.broadcasted_iota(jnp.int32, (8, WIDTH), 0) * BLOCK
        + lax.broadcasted_iota(jnp.int32, (8, WIDTH), 1)
        + half * HALF
    )

    def count(i, carry):
        end, start = carry
        end = end + len_ref[i]
        return end, jnp.where(positions >= end, end, start)

    _, doc_start = lax.fori_loop(
        0, len_ref.shape[0], count, (jnp.int32(0), jnp.zeros((8, WIDTH), jnp.int32))
    )
    starts[...] = doc_start - half * HALF
    acc1[...] = jnp.zeros_like(acc1)

    @pl.when(jnp.logical_not(has_old))
    def _():
        old_in[...] = jnp.zeros_like(old_in)

    @pl.when(jnp.logical_not(has_later))
    def _():
        relay_in[...] = jnp.zeros_like(relay_in)

    wait(own_in, own_sem)
    forward = remote(own_in, old_in, send.at[46], old_sem, place(2, y))

    @pl.when(has_later)
    def _():
        forward.start()

    push(own_in.at[1], far_v, far_sem.at[1], place(1, y))
    kv[:, HALF : 2 * HALF] = own_in[...]
    kt[:, HALF : 2 * HALF] = own_in[0].T

    @pl.when(has_old)
    def _():
        wait(old_in, old_sem)

    kv[:, 0:HALF] = old_in[...]
    kt[:, 0:HALF] = old_in[0].T

    row = lax.broadcasted_iota(jnp.int32, (CHUNK, PAIR), 0)
    token = lax.rem(lax.broadcasted_iota(jnp.int32, (CHUNK, PAIR), 1), WIDTH)

    def unpack(pair, part):
        wait(qg[pair][part], q_sem.at[2 * pair + part])
        for j in range(HEADS):
            x = qg[pair][part][j]
            rows = slice(j // 2 * PAIR, (j // 2 + 1) * PAIR)
            rows_of[pair, part, j % 2, rows] = jnp.concatenate([x[:, :WIDTH], x[:, WIDTH:]], axis=0)

    def unit(pair, j):
        k, u = j % 2, 2 * pair + j // 2
        rows = slice(j // 2 * PAIR, (j // 2 + 1) * PAIR)
        return k, u, rows_of.at[pair, 0, k, rows], rows_of.at[pair, 1, k, rows]

    def staged(ahead, work):
        ahead(0)
        for j in range(HEADS):
            if j + 1 < HEADS:
                ahead(j + 1)
            work(j)

    def first_of(j):
        line = starts[j : j + 1]
        return jnp.concatenate([line, line], axis=1)

    def softmax(first, chunks, base, e, diagonal):
        top = jnp.full((8, PAIR), FILL, jnp.float32)
        for c in range(chunks):
            rows = slice(c * CHUNK, (c + 1) * CHUNK)
            keep = row >= first - base(c)
            if diagonal and c >= chunks - BLOCK // CHUNK:
                keep = keep & (row + (c * CHUNK) % BLOCK <= token)
            s = jnp.where(keep, e[rows], FILL)
            e[rows] = s
            top = jnp.maximum(top, fold(s, jnp.max))
        top = jnp.max(top, axis=0, keepdims=True)
        total = jnp.zeros((8, PAIR), jnp.float32)
        for c in range(chunks):
            rows = slice(c * CHUNK, (c + 1) * CHUNK)
            x = jnp.exp((e[rows] - top) * SCALE)
            e[rows] = x
            total = total + fold(x, jnp.sum)
        return top, jnp.sum(total, axis=0, keepdims=True)

    def weighted(chunks, e, p):
        delta = jnp.zeros((8, PAIR), jnp.float32)
        for c in range(chunks):
            rows = slice(c * CHUNK, (c + 1) * CHUNK)
            delta = delta + fold(e[rows] * p[rows], jnp.sum)
        return jnp.sum(delta, axis=0, keepdims=True)

    def near_scores(pair):
        def ahead(j):
            k, u, q, g = unit(pair, j)
            e1[k][u] = contract_last(kv[0, j * BLOCK : j * BLOCK + NEAR], q[...])

        def work(j):
            k, u, q, g = unit(pair, j)

            def base(c):
                block = j + c * CHUNK // BLOCK
                start = block * BLOCK - 2 * HALF if block < HEADS else (block - HEADS) * BLOCK
                return start + (c * CHUNK) % BLOCK

            top, total = softmax(first_of(j), NEAR // CHUNK, base, e1[k].at[u], True)
            stat[k][u, 0:1] = top
            stat[k][u, 1:2] = total

        staged(ahead, work)

    def far_scores(pair):
        def ahead(j):
            k, u, q, g = unit(pair, j)
            e2[k][j // 2] = contract_last(far_k[...], q[...])

        def work(j):
            k, u, q, g = unit(pair, j)
            i, cols = j // 2, slice(j // 2 * PAIR, (j // 2 + 1) * PAIR)
            top2, total2 = softmax(first_of(j), HALF // CHUNK, lambda c: c * CHUNK - HALF, e2[k].at[i], False)
            top1, total1 = stat[k][u, 0:1], stat[k][u, 1:2]
            top = jnp.maximum(top1, top2)
            a1 = jnp.exp((top1 - top) * SCALE)
            a2 = jnp.exp((top2 - top) * SCALE)
            inverse = 1.0 / (a1 * total1 + a2 * total2)
            stat[k][u, 5:6] = a1 * inverse
            a2 = a2 * inverse
            for c in range(HALF // CHUNK):
                rows = slice(c * CHUNK, (c + 1) * CHUNK)
                p = e2[k][i, rows] * a2
                e2[k][i, rows] = p
                pr_far[k][rows, cols] = p.astype(jnp.bfloat16)

        staged(ahead, work)

    def near_values(pair):
        def ahead(j):
            k, u, q, g = unit(pair, j)
            p1[k][u] = contract_last(kv[1, j * BLOCK : j * BLOCK + NEAR], g[...])

        def work(j):
            k, u, q, g = unit(pair, j)
            stat[k][u, 4:5] = weighted(NEAR // CHUNK, e1[k].at[u], p1[k].at[u])

        staged(ahead, work)

    def far_values(pair):
        def ahead(j):
            k, u, q, g = unit(pair, j)
            p2[k][j // 2] = contract_last(far_v[...], g[...])

        def work(j):
            k, u, q, g = unit(pair, j)
            i, cols = j // 2, slice(j // 2 * PAIR, (j // 2 + 1) * PAIR)
            delta = stat[k][u, 5:6] * stat[k][u, 4:5] + weighted(HALF // CHUNK, e2[k].at[i], p2[k].at[i])
            stat[k][u, 6:7] = delta
            for c in range(HALF // CHUNK):
                rows = slice(c * CHUNK, (c + 1) * CHUNK)
                ds_far[k][rows, cols] = (e2[k][i, rows] * (p2[k][i, rows] - delta)).astype(jnp.bfloat16)

        staged(ahead, work)

    def far_queries(pair):
        for j in range(HEADS):
            k, u, q, g = unit(pair, j)
            dqt[k][u] = matmul(kt_far[...], ds_far[k][:, j // 2 * PAIR : (j // 2 + 1) * PAIR])

    def near_rows(pair, j, low, high):
        k, u = j % 2, 2 * pair + j // 2
        a1, delta = stat[k][u, 5:6], stat[k][u, 6:7]
        for c in range(low // CHUNK, high // CHUNK):
            rows = slice(c * CHUNK, (c + 1) * CHUNK)
            p = e1[k][u, rows] * a1
            ds1[j][pair, rows] = (p * (p1[k][u, rows] - delta)).astype(jnp.bfloat16)
            pr1[j][rows] = p.astype(jnp.bfloat16)

    def near_keys(pair, j, low, high):
        keys = slice(j * BLOCK + low, j * BLOCK + high)
        mine = slice(j // 2 * PAIR, (j // 2 + 1) * PAIR)
        acc1[0, keys] += matmul(ds1[j][pair, low:high], rows_of[pair, 0, j % 2, mine])
        acc1[1, keys] += matmul(pr1[j][low:high], rows_of[pair, 1, j % 2, mine])

    def old_work(pair):
        for j in range(HEADS):
            near_rows(pair, j, 0, HALF - j * BLOCK)
        for j in range(HEADS):
            near_keys(pair, j, 0, HALF - j * BLOCK)

    def own_work(pair):
        for j in range(HEADS):
            near_rows(pair, j, HALF - j * BLOCK, NEAR)
        for j in range(HEADS):
            near_keys(pair, j, HALF - j * BLOCK, NEAR)
            k, u = j % 2, 2 * pair + j // 2
            total = dqt[k][u] + matmul(kt[:, j * BLOCK : j * BLOCK + NEAR], ds1[j][pair])
            total = (total * SCALE).T.astype(jnp.bfloat16)
            dqs[pair][j] = jnp.concatenate([total[:BLOCK], total[BLOCK:]], axis=1)

    mine = pl.ds(pl.multiple_of(y * WIDTH, WIDTH), WIDTH)

    def send_far(part):
        for d in range(HEADS):
            j = row_at(d)
            rows = pl.ds(pl.multiple_of(j * BLOCK, BLOCK), BLOCK)
            push(far_out[part].at[rows], back.at[1, part, :, mine], back_sem.at[1], place(-1, j))

    def far_sum(pair, part, left):
        total = matmul(left[0][...], rows_of[pair, part, 0]) + matmul(left[1][...], rows_of[pair, part, 1])
        if pair == 0:
            acc2[part] = total
        else:
            far_out[part][...] = (acc2[part] + total).astype(jnp.bfloat16)
            send_far(part)

    def send_queries(pair):
        dst = dq_ref.at[:, pl.ds(pl.multiple_of(y * SHARE * WIDTH + pair * PAIR, PAIR), PAIR)]
        for d in range(HEADS):
            j = row_at(d)
            if d == 0:
                pltpu.make_async_copy(dqs[pair].at[j], dst, dq_sem).start()
            else:
                push(dqs[pair].at[j], dst, dq_sem, place(0, j))

    for pair in range(2):
        unpack(pair, 0)
        near_scores(pair)
        if pair == 0:
            unpack(pair, 1)
            near_values(pair)
            wait(far_k, far_sem.at[0])
            kt_far[...] = far_k[...].T
            far_scores(pair)
            far_sum(pair, 1, pr_far)
            wait(far_v, far_sem.at[1])
        else:
            far_scores(pair)
            unpack(pair, 1)
            far_sum(pair, 1, pr_far)
            near_values(pair)
        far_values(pair)
        if pair == 0:
            far_queries(pair)
        far_sum(pair, 0, ds_far)

    old_work(0)
    old_work(1)
    relay_out[...] = acc1[:, 0:HALF].astype(jnp.bfloat16)
    backward = remote(relay_out, relay_in, send.at[47], relay_sem, place(-2, y))

    @pl.when(has_old)
    def _():
        backward.start()

    own_work(0)
    send_queries(0)
    far_queries(1)
    own_work(1)
    send_queries(1)
    @pl.when(has_later)
    def _():
        wait(relay_in, relay_sem)

    own_out[...] = (acc1[:, HALF : 2 * HALF] + relay_in[...].astype(jnp.float32)).astype(jnp.bfloat16)
    for d in range(HEADS):
        j = row_at(d)
        rows = pl.ds(pl.multiple_of(j * BLOCK, BLOCK), BLOCK)
        if d == 0:
            pltpu.make_async_copy(own_out.at[:, rows], back.at[0, :, :, mine], back_sem.at[0]).start()
        else:
            push(own_out.at[:, rows], back.at[0, :, :, mine], back_sem.at[0], place(0, j))
    wait(back.at[0], back_sem.at[0])
    wait(back.at[1], back_sem.at[1])
    wait(dq_ref, dq_sem)
    for copy in started:
        copy.wait_send()

    @pl.when(has_later)
    def _():
        forward.wait_send()

    @pl.when(has_old)
    def _():
        backward.wait_send()


def finish(dq_in, back, dq_ref, dk_ref, dv_ref):
    dq_ref[...] = dq_in[...]
    total = back[0].astype(jnp.float32) + back[1].astype(jnp.float32)
    dk_ref[...] = (total[0] * SCALE).astype(jnp.bfloat16)
    dv_ref[...] = total[1].astype(jnp.bfloat16)


def local(queries, key_vectors, value_vectors, output_gradient, doc_lengths):
    low, full = jnp.bfloat16, jnp.float32
    wide = jax.ShapeDtypeStruct((BLOCK, HEADS * SHARE * WIDTH), low)
    narrow = jax.ShapeDtypeStruct((BLOCK, HEADS * WIDTH), low)
    shares = jax.ShapeDtypeStruct((2, 2, BLOCK, HEADS * WIDTH), low)
    anywhere = pl.BlockSpec(memory_space=pl.ANY)
    near = pl.BlockSpec(memory_space=pltpu.VMEM)
    query_grad, back = pl.pallas_call(
        kernel,
        out_shape=(wide, shares),
        in_specs=[anywhere] * 4 + [pl.BlockSpec(memory_space=pltpu.SMEM)],
        out_specs=(anywhere, anywhere),
        scratch_shapes=[
            pltpu.VMEM((2, 2 * HALF, WIDTH), low),
            pltpu.VMEM((2, HALF, WIDTH), low),
            pltpu.VMEM((HALF, WIDTH), low),
            pltpu.VMEM((HALF, WIDTH), low),
            pltpu.VMEM((2, HALF, WIDTH), low),
            pltpu.VMEM((WIDTH, 2 * HALF), low),
            pltpu.VMEM((WIDTH, HALF), low),
            pltpu.VMEM((HEADS, BLOCK, PAIR), low),
            pltpu.VMEM((HEADS, BLOCK, PAIR), low),
            pltpu.VMEM((HEADS, BLOCK, PAIR), low),
            pltpu.VMEM((HEADS, BLOCK, PAIR), low),
            pltpu.VMEM((2, 2, 2, 2 * PAIR, WIDTH), low),
            pltpu.VMEM((8, WIDTH), jnp.int32),
            pltpu.VMEM((4, NEAR, PAIR), full),
            pltpu.VMEM((4, NEAR, PAIR), full),
            pltpu.VMEM((4, NEAR, PAIR), full),
            pltpu.VMEM((4, NEAR, PAIR), full),
            pltpu.VMEM((2, HALF, PAIR), full),
            pltpu.VMEM((2, HALF, PAIR), full),
            pltpu.VMEM((2, HALF, PAIR), full),
            pltpu.VMEM((2, HALF, PAIR), full),
            pltpu.VMEM((HALF, 2 * PAIR), low),
            pltpu.VMEM((HALF, 2 * PAIR), low),
            pltpu.VMEM((HALF, 2 * PAIR), low),
            pltpu.VMEM((HALF, 2 * PAIR), low),
            pltpu.VMEM((2, NEAR, PAIR), low),
            pltpu.VMEM((2, NEAR, PAIR), low),
            pltpu.VMEM((2, NEAR, PAIR), low),
            pltpu.VMEM((2, NEAR, PAIR), low),
            pltpu.VMEM((NEAR, PAIR), low),
            pltpu.VMEM((NEAR, PAIR), low),
            pltpu.VMEM((NEAR, PAIR), low),
            pltpu.VMEM((NEAR, PAIR), low),
            pltpu.VMEM((4, 8, PAIR), full),
            pltpu.VMEM((4, 8, PAIR), full),
            pltpu.VMEM((4, WIDTH, PAIR), full),
            pltpu.VMEM((4, WIDTH, PAIR), full),
            pltpu.VMEM((2, 2 * HALF, WIDTH), full),
            pltpu.VMEM((2, HALF, WIDTH), full),
            pltpu.VMEM((HEADS, BLOCK, PAIR), low),
            pltpu.VMEM((HEADS, BLOCK, PAIR), low),
            pltpu.VMEM((HALF, WIDTH), low),
            pltpu.VMEM((HALF, WIDTH), low),
            pltpu.VMEM((2, HALF, WIDTH), low),
            pltpu.VMEM((2, HALF, WIDTH), low),
            pltpu.VMEM((2, HALF, WIDTH), low),
            pltpu.SemaphoreType.DMA((48,)),
            pltpu.SemaphoreType.DMA,
            pltpu.SemaphoreType.DMA((2,)),
            pltpu.SemaphoreType.DMA,
            pltpu.SemaphoreType.DMA((4,)),
            pltpu.SemaphoreType.DMA,
            pltpu.SemaphoreType.DMA((2,)),
            pltpu.SemaphoreType.DMA,
        ],
        compiler_params=pltpu.CompilerParams(
            collective_id=0, has_side_effects=True, vmem_limit_bytes=60 << 20
        ),
        cost_estimate=pl.CostEstimate(flops=3 << 30, bytes_accessed=3 << 20, transcendentals=3 << 20),
    )(queries, key_vectors, value_vectors, output_gradient, doc_lengths)
    return pl.pallas_call(
        finish,
        out_shape=(wide, narrow, narrow),
        in_specs=[near, near],
        out_specs=(near, near, near),
        compiler_params=pltpu.CompilerParams(vmem_limit_bytes=60 << 20),
    )(query_grad, back)


def solution(mesh):
    rows = P(("pb", "kv"), None)
    return jax.shard_map(
        local, mesh=mesh, in_specs=(rows, rows, rows, rows, P()), out_specs=(rows, rows, rows), check_vma=False
    )
```

```python
import jax
import jax.numpy as jnp
from jax import lax
from jax.experimental import pallas as pl
from jax.experimental.pallas import tpu as pltpu
from jax.sharding import PartitionSpec as P

MESH = pl.DeviceIdType.MESH
HEADS = 4
SHARE = 4
WIDTH = 128
BLOCK = 128
HALF = HEADS * BLOCK
NEAR = 5 * BLOCK
PAIR = 2 * WIDTH
HALVES = 64
CHUNK = 64
SCALE = WIDTH**-0.5
FILL = -1e30


def contract_last(left, right):
    return lax.dot_general(left, right, (((1,), (1,)), ((), ())), preferred_element_type=jnp.float32)


def matmul(left, right):
    return jnp.dot(left, right, preferred_element_type=jnp.float32)


def fold(x, op):
    return op(x.reshape(x.shape[0] // 8, 8, x.shape[1]), axis=0)


def wait(ref, sem):
    pltpu.make_async_copy(ref, ref, sem).wait()


def kernel(
    q_ref, k_ref, v_ref, g_ref, len_ref,
    dq_ref, back,
    kv, own_in, far_k, far_v, old_in, kt, kt_far, q0, g0, q1, g1, rows_of, starts,
    e1a, e1b, p1a, p1b, e2a, e2b, p2a, p2b, ds_fa, ds_fb, pr_fa, pr_fb, ds_0, ds_1, ds_2, ds_3, pr_0, pr_1, pr_2, pr_3,
    stat_a, stat_b, dqt_a, dqt_b, acc1, acc2, dqs0, dqs1, far_ok, far_ov, relay_out, relay_in, own_out,
    send, own_sem, far_sem, old_sem, q_sem, relay_sem, back_sem, dq_sem,
):
    dqs = (dqs0, dqs1)
    qg, e1, p1, e2, p2 = ((q0, g0), (q1, g1)), (e1a, e1b), (p1a, p1b), (e2a, e2b), (p2a, p2b)
    ds1, pr1 = (ds_0, ds_1, ds_2, ds_3), (pr_0, pr_1, pr_2, pr_3)
    stat, dqt = (stat_a, stat_b), (dqt_a, dqt_b)
    ds_far, pr_far, far_out = (ds_fa, ds_fb), (pr_fa, pr_fb), (far_ok, far_ov)
    pb, column = lax.axis_index("pb"), lax.axis_index("kv")
    half = 2 * pb + column // HEADS
    y = lax.rem(column, HEADS)
    has_old = half >= 2
    has_later = half < HALVES - 2

    def place(shift, row):
        there = lax.rem(half + shift + HALVES, HALVES)
        return (there // 2, lax.rem(there, 2) * HEADS + row)

    def row_at(step):
        return lax.rem(y + step, HEADS)

    partners = [place(0, row_at(d)) for d in (1, 2, 3)]
    partners += [place(s, row_at(d)) for s in (1, -1) for d in range(HEADS)]
    barrier = pltpu.get_barrier_semaphore()
    for device in partners:
        pl.semaphore_signal(barrier, inc=1, device_id=device, device_id_type=MESH)

    @pl.when(has_later)
    def _():
        pl.semaphore_signal(barrier, inc=1, device_id=place(2, y), device_id_type=MESH)

    @pl.when(has_old)
    def _():
        pl.semaphore_signal(barrier, inc=1, device_id=place(-2, y), device_id_type=MESH)

    pl.semaphore_wait(barrier, len(partners) + has_old.astype(jnp.int32) + has_later.astype(jnp.int32))

    started = []

    def remote(src, dst, send_sem, recv_sem, device):
        return pltpu.make_async_remote_copy(
            src_ref=src, dst_ref=dst, send_sem=send_sem, recv_sem=recv_sem, device_id=device, device_id_type=MESH
        )

    def push(src, dst, recv_sem, device):
        copy = remote(src, dst, send.at[len(started)], recv_sem, device)
        copy.start()
        started.append(copy)

    def share(ref, part, d):
        h = row_at(d)
        return h, ref.at[:, pl.ds(pl.multiple_of(h * WIDTH, WIDTH), WIDTH)]

    slot = pl.ds(pl.multiple_of(y * BLOCK, BLOCK), BLOCK)
    for part, ref in enumerate((k_ref, v_ref)):
        for d in range(HEADS):
            h, src = share(ref, part, d)
            if d == 0:
                pltpu.make_async_copy(src, own_in.at[part, slot], own_sem).start()
            else:
                push(src, own_in.at[part, slot], own_sem, place(0, h))
    for ref, far, sem in ((k_ref, far_k, far_sem.at[0]), (v_ref, far_v, far_sem.at[1])):
        for d in range(HEADS):
            h, src = share(ref, 0, d)
            push(src, far.at[slot], sem, place(1, h))
    for pair in range(2):
        for part, ref in enumerate((q_ref, g_ref)):
            for d in range(HEADS):
                h = row_at(d)
                cols = pl.ds(pl.multiple_of(h * SHARE * WIDTH + pair * PAIR, PAIR), PAIR)
                dst, sem = qg[pair][part].at[y], q_sem.at[2 * pair + part]
                if d == 0:
                    pltpu.make_async_copy(ref.at[:, cols], dst, sem).start()
                else:
                    push(ref.at[:, cols], dst, sem, place(0, h))

    positions = (
        lax.broadcasted_iota(jnp.int32, (8, WIDTH), 0) * BLOCK
        + lax.broadcasted_iota(jnp.int32, (8, WIDTH), 1)
        + half * HALF
    )

    def count(i, carry):
        end, start = carry
        end = end + len_ref[i]
        return end, jnp.where(positions >= end, end, start)

    _, doc_start = lax.fori_loop(
        0, len_ref.shape[0], count, (jnp.int32(0), jnp.zeros((8, WIDTH), jnp.int32))
    )
    starts[...] = doc_start - half * HALF
    acc1[...] = jnp.zeros_like(acc1)

    @pl.when(jnp.logical_not(has_old))
    def _():
        old_in[...] = jnp.zeros_like(old_in)

    @pl.when(jnp.logical_not(has_later))
    def _():
        relay_in[...] = jnp.zeros_like(relay_in)

    wait(own_in, own_sem)
    forward = remote(own_in, old_in, send.at[46], old_sem, place(2, y))

    @pl.when(has_later)
    def _():
        forward.start()

    kv[:, HALF : 2 * HALF] = own_in[...]
    kt[:, HALF : 2 * HALF] = own_in[0].T

    row = lax.broadcasted_iota(jnp.int32, (CHUNK, PAIR), 0)
    token = lax.rem(lax.broadcasted_iota(jnp.int32, (CHUNK, PAIR), 1), WIDTH)

    def unpack(pair, part):
        wait(qg[pair][part], q_sem.at[2 * pair + part])
        for j in range(HEADS):
            x = qg[pair][part][j]
            rows = slice(j // 2 * PAIR, (j // 2 + 1) * PAIR)
            rows_of[pair, part, j % 2, rows] = jnp.concatenate([x[:, :WIDTH], x[:, WIDTH:]], axis=0)

    def unit(pair, j):
        k, u = j % 2, 2 * pair + j // 2
        rows = slice(j // 2 * PAIR, (j // 2 + 1) * PAIR)
        return k, u, rows_of.at[pair, 0, k, rows], rows_of.at[pair, 1, k, rows]

    def staged(ahead, work):
        ahead(0)
        for j in range(HEADS):
            if j + 1 < HEADS:
                ahead(j + 1)
            work(j)

    def first_of(j):
        line = starts[j : j + 1]
        return jnp.concatenate([line, line], axis=1)

    def softmax(first, pieces):
        top = jnp.full((8, PAIR), FILL, jnp.float32)
        for e, rows, base, diagonal in pieces:
            for r in range(rows.start, rows.stop, CHUNK):
                part = slice(r, r + CHUNK)
                keep = row >= first - (base + r - rows.start)
                if diagonal and r >= rows.stop - BLOCK:
                    keep = keep & (row + (r - rows.stop + BLOCK) <= token)
                s = jnp.where(keep, e[part], FILL)
                e[part] = s
                top = jnp.maximum(top, fold(s, jnp.max))
        top = jnp.max(top, axis=0, keepdims=True)
        total = jnp.zeros((8, PAIR), jnp.float32)
        for e, rows, base, diagonal in pieces:
            for r in range(rows.start, rows.stop, CHUNK):
                part = slice(r, r + CHUNK)
                x = jnp.exp((e[part] - top) * SCALE)
                e[part] = x
                total = total + fold(x, jnp.sum)
        return top, jnp.sum(total, axis=0, keepdims=True)

    def weighted(rows, e, p):
        delta = jnp.zeros((8, PAIR), jnp.float32)
        for r in range(rows.start, rows.stop, CHUNK):
            part = slice(r, r + CHUNK)
            delta = delta + fold(e[part] * p[part], jnp.sum)
        return jnp.sum(delta, axis=0, keepdims=True)

    def old_rows(j):
        return slice(0, HALF - j * BLOCK)

    def own_rows(j):
        return slice(HALF - j * BLOCK, NEAR)

    def own_scores(pair):
        def ahead(j):
            k, u, q, g = unit(pair, j)
            e1[k][u, own_rows(j)] = contract_last(kv[0, HALF : HALF + (j + 1) * BLOCK], q[...])

        def work(j):
            k, u, q, g = unit(pair, j)
            top, total = softmax(first_of(j), [(e1[k].at[u], own_rows(j), 0, True)])
            stat[k][u, 0:1] = top
            stat[k][u, 1:2] = total

        staged(ahead, work)

    def far_scores(pair):
        def ahead(j):
            k, u, q, g = unit(pair, j)
            e1[k][u, old_rows(j)] = contract_last(kv[0, j * BLOCK : HALF], q[...])
            e2[k][j // 2] = contract_last(far_k[...], q[...])

        def work(j):
            k, u, q, g = unit(pair, j)
            i, cols = j // 2, slice(j // 2 * PAIR, (j // 2 + 1) * PAIR)
            pieces = [
                (e1[k].at[u], old_rows(j), j * BLOCK - 2 * HALF, False),
                (e2[k].at[i], slice(0, HALF), -HALF, False),
            ]
            top2, total2 = softmax(first_of(j), pieces)
            top1, total1 = stat[k][u, 0:1], stat[k][u, 1:2]
            top = jnp.maximum(top1, top2)
            a1 = jnp.exp((top1 - top) * SCALE)
            a2 = jnp.exp((top2 - top) * SCALE)
            inverse = 1.0 / (a1 * total1 + a2 * total2)
            a2 = a2 * inverse
            stat[k][u, 2:3] = a2
            stat[k][u, 5:6] = a1 * inverse
            for c in range(HALF // CHUNK):
                rows = slice(c * CHUNK, (c + 1) * CHUNK)
                p = e2[k][i, rows] * a2
                e2[k][i, rows] = p
                pr_far[k][rows, cols] = p.astype(jnp.bfloat16)

        staged(ahead, work)

    def own_values(pair):
        def ahead(j):
            k, u, q, g = unit(pair, j)
            p1[k][u, own_rows(j)] = contract_last(kv[1, HALF : HALF + (j + 1) * BLOCK], g[...])

        def work(j):
            k, u, q, g = unit(pair, j)
            stat[k][u, 4:5] = weighted(own_rows(j), e1[k].at[u], p1[k].at[u])

        staged(ahead, work)

    def old_values(pair):
        def ahead(j):
            k, u, q, g = unit(pair, j)
            p1[k][u, old_rows(j)] = contract_last(kv[1, j * BLOCK : HALF], g[...])

        def work(j):
            k, u, q, g = unit(pair, j)
            stat[k][u, 3:4] = weighted(old_rows(j), e1[k].at[u], p1[k].at[u])

        staged(ahead, work)

    def far_values(pair):
        def ahead(j):
            k, u, q, g = unit(pair, j)
            p2[k][j // 2] = contract_last(far_v[...], g[...])

        def work(j):
            k, u, q, g = unit(pair, j)
            i, cols = j // 2, slice(j // 2 * PAIR, (j // 2 + 1) * PAIR)
            delta = stat[k][u, 5:6] * stat[k][u, 4:5] + stat[k][u, 2:3] * stat[k][u, 3:4]
            delta = delta + weighted(slice(0, HALF), e2[k].at[i], p2[k].at[i])
            stat[k][u, 6:7] = delta
            for c in range(HALF // CHUNK):
                rows = slice(c * CHUNK, (c + 1) * CHUNK)
                ds_far[k][rows, cols] = (e2[k][i, rows] * (p2[k][i, rows] - delta)).astype(jnp.bfloat16)

        staged(ahead, work)

    def far_queries(pair):
        for j in range(HEADS):
            k, u, q, g = unit(pair, j)
            dqt[k][u] = matmul(kt_far[...], ds_far[k][:, j // 2 * PAIR : (j // 2 + 1) * PAIR])

    def near_rows(pair, j, low, high, line):
        k, u = j % 2, 2 * pair + j // 2
        a1, delta = stat[k][u, line : line + 1], stat[k][u, 6:7]
        for c in range(low // CHUNK, high // CHUNK):
            rows = slice(c * CHUNK, (c + 1) * CHUNK)
            p = e1[k][u, rows] * a1
            ds1[j][pair, rows] = (p * (p1[k][u, rows] - delta)).astype(jnp.bfloat16)
            pr1[j][rows] = p.astype(jnp.bfloat16)

    def near_keys(pair, j, low, high):
        keys = slice(j * BLOCK + low, j * BLOCK + high)
        mine = slice(j // 2 * PAIR, (j // 2 + 1) * PAIR)
        acc1[0, keys] += matmul(ds1[j][pair, low:high], rows_of[pair, 0, j % 2, mine])
        acc1[1, keys] += matmul(pr1[j][low:high], rows_of[pair, 1, j % 2, mine])

    def old_work(pair):
        for j in range(HEADS):
            near_rows(pair, j, 0, HALF - j * BLOCK, 2)
        for j in range(HEADS):
            near_keys(pair, j, 0, HALF - j * BLOCK)

    def own_work(pair):
        for j in range(HEADS):
            near_rows(pair, j, HALF - j * BLOCK, NEAR, 5)
        for j in range(HEADS):
            near_keys(pair, j, HALF - j * BLOCK, NEAR)
            k, u = j % 2, 2 * pair + j // 2
            total = dqt[k][u] + matmul(kt[:, j * BLOCK : j * BLOCK + NEAR], ds1[j][pair])
            total = (total * SCALE).T.astype(jnp.bfloat16)
            dqs[pair][j] = jnp.concatenate([total[:BLOCK], total[BLOCK:]], axis=1)

    mine = pl.ds(pl.multiple_of(y * WIDTH, WIDTH), WIDTH)

    def send_far(part):
        for d in range(HEADS):
            j = row_at(d)
            rows = pl.ds(pl.multiple_of(j * BLOCK, BLOCK), BLOCK)
            push(far_out[part].at[rows], back.at[1, part, :, mine], back_sem.at[1], place(-1, j))

    def far_sum(pair, part, left):
        total = matmul(left[0][...], rows_of[pair, part, 0]) + matmul(left[1][...], rows_of[pair, part, 1])
        if pair == 0:
            acc2[part] = total
        else:
            far_out[part][...] = (acc2[part] + total).astype(jnp.bfloat16)
            send_far(part)

    def send_queries(pair):
        dst = dq_ref.at[:, pl.ds(pl.multiple_of(y * SHARE * WIDTH + pair * PAIR, PAIR), PAIR)]
        for d in range(HEADS):
            j = row_at(d)
            if d == 0:
                pltpu.make_async_copy(dqs[pair].at[j], dst, dq_sem).start()
            else:
                push(dqs[pair].at[j], dst, dq_sem, place(0, j))

    for pair in range(2):
        unpack(pair, 0)
        own_scores(pair)
        if pair == 0:
            unpack(pair, 1)
            own_values(pair)

            @pl.when(has_old)
            def _():
                wait(old_in, old_sem)

            kv[:, 0:HALF] = old_in[...]
            kt[:, 0:HALF] = old_in[0].T

            wait(far_k, far_sem.at[0])
            kt_far[...] = far_k[...].T
            far_scores(pair)
            far_sum(pair, 1, pr_far)
            old_values(pair)
            wait(far_v, far_sem.at[1])
        else:
            far_scores(pair)
            old_work(0)
            own_work(0)
            unpack(pair, 1)
            send_queries(0)
            far_sum(pair, 1, pr_far)
            own_values(pair)
            old_values(pair)
        far_values(pair)
        if pair == 0:
            far_queries(pair)
        if pair == 0:
            far_sum(pair, 0, ds_far)

    old_work(1)
    relay_out[...] = acc1[:, 0:HALF].astype(jnp.bfloat16)
    backward = remote(relay_out, relay_in, send.at[47], relay_sem, place(-2, y))

    @pl.when(has_old)
    def _():
        backward.start()

    far_sum(1, 0, ds_far)

    far_queries(1)
    own_work(1)
    send_queries(1)
    @pl.when(has_later)
    def _():
        wait(relay_in, relay_sem)

    own_out[...] = (acc1[:, HALF : 2 * HALF] + relay_in[...].astype(jnp.float32)).astype(jnp.bfloat16)
    for d in range(HEADS):
        j = row_at(d)
        rows = pl.ds(pl.multiple_of(j * BLOCK, BLOCK), BLOCK)
        if d == 0:
            pltpu.make_async_copy(own_out.at[:, rows], back.at[0, :, :, mine], back_sem.at[0]).start()
        else:
            push(own_out.at[:, rows], back.at[0, :, :, mine], back_sem.at[0], place(0, j))
    wait(back.at[0], back_sem.at[0])
    wait(back.at[1], back_sem.at[1])
    wait(dq_ref, dq_sem)
    for copy in started:
        copy.wait_send()

    @pl.when(has_later)
    def _():
        forward.wait_send()

    @pl.when(has_old)
    def _():
        backward.wait_send()


def finish(dq_in, back, dq_ref, dk_ref, dv_ref):
    dq_ref[...] = dq_in[...]
    total = back[0].astype(jnp.float32) + back[1].astype(jnp.float32)
    dk_ref[...] = (total[0] * SCALE).astype(jnp.bfloat16)
    dv_ref[...] = total[1].astype(jnp.bfloat16)


def local(queries, key_vectors, value_vectors, output_gradient, doc_lengths):
    low, full = jnp.bfloat16, jnp.float32
    wide = jax.ShapeDtypeStruct((BLOCK, HEADS * SHARE * WIDTH), low)
    narrow = jax.ShapeDtypeStruct((BLOCK, HEADS * WIDTH), low)
    shares = jax.ShapeDtypeStruct((2, 2, BLOCK, HEADS * WIDTH), low)
    anywhere = pl.BlockSpec(memory_space=pl.ANY)
    near = pl.BlockSpec(memory_space=pltpu.VMEM)
    query_grad, back = pl.pallas_call(
        kernel,
        out_shape=(wide, shares),
        in_specs=[anywhere] * 4 + [pl.BlockSpec(memory_space=pltpu.SMEM)],
        out_specs=(anywhere, anywhere),
        scratch_shapes=[
            pltpu.VMEM((2, 2 * HALF, WIDTH), low),
            pltpu.VMEM((2, HALF, WIDTH), low),
            pltpu.VMEM((HALF, WIDTH), low),
            pltpu.VMEM((HALF, WIDTH), low),
            pltpu.VMEM((2, HALF, WIDTH), low),
            pltpu.VMEM((WIDTH, 2 * HALF), low),
            pltpu.VMEM((WIDTH, HALF), low),
            pltpu.VMEM((HEADS, BLOCK, PAIR), low),
            pltpu.VMEM((HEADS, BLOCK, PAIR), low),
            pltpu.VMEM((HEADS, BLOCK, PAIR), low),
            pltpu.VMEM((HEADS, BLOCK, PAIR), low),
            pltpu.VMEM((2, 2, 2, 2 * PAIR, WIDTH), low),
            pltpu.VMEM((8, WIDTH), jnp.int32),
            pltpu.VMEM((4, NEAR, PAIR), full),
            pltpu.VMEM((4, NEAR, PAIR), full),
            pltpu.VMEM((4, NEAR, PAIR), full),
            pltpu.VMEM((4, NEAR, PAIR), full),
            pltpu.VMEM((2, HALF, PAIR), full),
            pltpu.VMEM((2, HALF, PAIR), full),
            pltpu.VMEM((2, HALF, PAIR), full),
            pltpu.VMEM((2, HALF, PAIR), full),
            pltpu.VMEM((HALF, 2 * PAIR), low),
            pltpu.VMEM((HALF, 2 * PAIR), low),
            pltpu.VMEM((HALF, 2 * PAIR), low),
            pltpu.VMEM((HALF, 2 * PAIR), low),
            pltpu.VMEM((2, NEAR, PAIR), low),
            pltpu.VMEM((2, NEAR, PAIR), low),
            pltpu.VMEM((2, NEAR, PAIR), low),
            pltpu.VMEM((2, NEAR, PAIR), low),
            pltpu.VMEM((NEAR, PAIR), low),
            pltpu.VMEM((NEAR, PAIR), low),
            pltpu.VMEM((NEAR, PAIR), low),
            pltpu.VMEM((NEAR, PAIR), low),
            pltpu.VMEM((4, 8, PAIR), full),
            pltpu.VMEM((4, 8, PAIR), full),
            pltpu.VMEM((4, WIDTH, PAIR), full),
            pltpu.VMEM((4, WIDTH, PAIR), full),
            pltpu.VMEM((2, 2 * HALF, WIDTH), full),
            pltpu.VMEM((2, HALF, WIDTH), full),
            pltpu.VMEM((HEADS, BLOCK, PAIR), low),
            pltpu.VMEM((HEADS, BLOCK, PAIR), low),
            pltpu.VMEM((HALF, WIDTH), low),
            pltpu.VMEM((HALF, WIDTH), low),
            pltpu.VMEM((2, HALF, WIDTH), low),
            pltpu.VMEM((2, HALF, WIDTH), low),
            pltpu.VMEM((2, HALF, WIDTH), low),
            pltpu.SemaphoreType.DMA((48,)),
            pltpu.SemaphoreType.DMA,
            pltpu.SemaphoreType.DMA((2,)),
            pltpu.SemaphoreType.DMA,
            pltpu.SemaphoreType.DMA((4,)),
            pltpu.SemaphoreType.DMA,
            pltpu.SemaphoreType.DMA((2,)),
            pltpu.SemaphoreType.DMA,
        ],
        compiler_params=pltpu.CompilerParams(
            collective_id=0, has_side_effects=True, vmem_limit_bytes=60 << 20
        ),
        cost_estimate=pl.CostEstimate(flops=3 << 30, bytes_accessed=3 << 20, transcendentals=3 << 20),
    )(queries, key_vectors, value_vectors, output_gradient, doc_lengths)
    return pl.pallas_call(
        finish,
        out_shape=(wide, narrow, narrow),
        in_specs=[near, near],
        out_specs=(near, near, near),
        compiler_params=pltpu.CompilerParams(vmem_limit_bytes=60 << 20),
    )(query_grad, back)


def solution(mesh):
    rows = P(("pb", "kv"), None)
    return jax.shard_map(
        local, mesh=mesh, in_specs=(rows, rows, rows, rows, P()), out_specs=(rows, rows, rows), check_vma=False
    )
```
